32 devices in a mesh: dp: 8 (over z, y), ctx: 4 (over x, core).
Axes of the slice: x: 2, y: 2, z: 4, core: 2. Of those that a mesh axis runs over, the one named last changes fastest.
Arguments:
- tokens: bfloat16 [8192, 2048], P(('dp', 'ctx')), may hold values from -6 to 6
- segments: int32 [8192], P(('dp', 'ctx')), may hold values from 0 to 2, as said below
- positions: int32 [8192], P(('dp', 'ctx')), may hold values from 0 to 1023, as said below
- out_grad: bfloat16 [8192, 2048], P(('dp', 'ctx')), may hold values from -6 to 6
- ln1_gain: bfloat16 [2048], P(('dp', 'ctx')), may hold values from 0.5 to 1.5
- ln1_bias: bfloat16 [2048], P(('dp', 'ctx')), may hold values from -1 to 1
- qkv_weight: bfloat16 [2048, 6144], P(('dp', 'ctx')), may hold values from -0.125 to 0.125
- qkv_bias: bfloat16 [2048, 3], P(('dp', 'ctx')), may hold values from -1.5 to 1.5
- o_weight: bfloat16 [2048, 2048], P(('dp', 'ctx')), may hold values from -0.5 to 0.5
- ln2_gain: bfloat16 [2048], P(('dp', 'ctx')), may hold values from 0.5 to 1.5
- ln2_bias: bfloat16 [2048], P(('dp', 'ctx')), may hold values from -1 to 1
- gate_weight: bfloat16 [2048, 5632], P(('dp', 'ctx')), may hold values from -0.125 to 0.125
- up_weight: bfloat16 [2048, 5632], P(('dp', 'ctx')), may hold values from -0.125 to 0.125
- down_weight: bfloat16 [2048, 5632], P(('dp', 'ctx')), may hold values from -0.078125 to 0.078125
Outputs:
- output: bfloat16 [8192, 2048], P(('dp', 'ctx'))
- input_grad: bfloat16 [8192, 2048], P(('dp', 'ctx'))
- ln1_gain_grad: float32 [2048], P(('dp', 'ctx'))
- ln1_bias_grad: float32 [2048], P(('dp', 'ctx'))
- qkv_weight_grad: float32 [2048, 6144], P(('dp', 'ctx'))
- qkv_bias_grad: float32 [2048, 3], P(('dp', 'ctx'))
- o_weight_grad: float32 [2048, 2048], P(('dp', 'ctx'))
- ln2_gain_grad: float32 [2048], P(('dp', 'ctx'))
- ln2_bias_grad: float32 [2048], P(('dp', 'ctx'))
- gate_weight_grad: float32 [2048, 5632], P(('dp', 'ctx'))
- up_weight_grad: float32 [2048, 5632], P(('dp', 'ctx'))
- down_weight_grad: float32 [2048, 5632], P(('dp', 'ctx'))
The draws below stay inside these ranges and needn't reach their ends.
Inputs may be any that keep to these rules, and one draw needn't show every extreme that they name: `segments`: within each pack of 1024 consecutive tokens the numbers never fall, and the first token of a pack has number 0. Within a run of equal segment numbers inside a pack, positions rise by one from token to token; the first token of every pack has position 0.
All inputs are finite; a program needn't handle non-finite values.
Results may differ from the reference program's by a relative error of at most 0.014.
Values may be sent and summed in bfloat16 or wider, within the bound.
No kernel may reach another device: no remote copies, remote signals or barrier semaphores. Data moves between devices by JAX's collectives and lax.ppermute only.
A program may use at most 832 MiB of HBM per device.

```python
import jax
import jax.numpy as jnp
from jax import lax

D = 2048
HEADS = 32
HEAD_DIM = 64
ROT_DIMS = 16
FF = 5632
TOK_DEV = 256
SEQ = 1024
TOKENS = 8192


def pack_cuts(key):
    pack_count = TOKENS // SEQ
    first_key, last_key = jax.random.split(key)
    first_cut = jax.random.randint(first_key, (pack_count, 1), 1, TOK_DEV // 2 + 1)
    last_cut = SEQ - jax.random.randint(last_key, (pack_count, 1), 1, TOK_DEV // 2 + 1)
    return (first_cut, last_cut)


def draw_segments(key, part):
    first_cut, last_cut = pack_cuts(key)
    offsets = jnp.arange(SEQ, dtype=jnp.int32)[None, :]
    labels = (offsets >= first_cut).astype(jnp.int32) + (offsets >= last_cut).astype(jnp.int32)
    return labels.reshape(TOKENS)


def draw_positions(key, part):
    first_cut, last_cut = pack_cuts(key)
    key = jax.random.fold_in(key, 12)
    pack_count = TOKENS // SEQ
    middle_room = SEQ - (last_cut - first_cut) + 1
    middle_start = jax.random.randint(key, (pack_count, 1), 0, middle_room)
    offsets = jnp.arange(SEQ, dtype=jnp.int32)[None, :]
    in_middle = offsets >= first_cut
    in_last = offsets >= last_cut
    seg_begin = jnp.where(in_last, last_cut, jnp.where(in_middle, first_cut, 0))
    seg_offset = jnp.where(in_last, last_cut, jnp.where(in_middle, middle_start, 0))
    return (offsets - seg_begin + seg_offset).astype(jnp.int32).reshape(TOKENS)


def spiked(values, rng, source, target, blocks, factor):
    owner, partner = [(jnp.arange(values.shape[position]) // (values.shape[position] // blocks)).reshape([-1 if axis == position else 1 for axis in range(values.ndim)]) for position in (source, target)]
    chosen = jax.random.permutation(rng, blocks)[partner]
    strong = (owner == chosen) | (owner == (partner + blocks // 2) % blocks)
    return jnp.where(strong, factor * values, values)


def level_of(own_key, shape, shards, low, high):
    gain, own = 1.0, jax.random.fold_in(own_key, 6)
    for axis_at, shards_of in shards:
        draws = jnp.exp(jax.random.uniform(jax.random.fold_in(own, axis_at), (shards_of,), jnp.float32, low / len(shards), high / len(shards)))
        gain = gain * jnp.repeat(draws, shape[axis_at] // shards_of).reshape([-1 if axis == axis_at else 1 for axis in range(len(shape))])
    return gain


def normal_values(own_key, dims, scale, most, shards=(), held_as=jnp.bfloat16):
    drawn = scale * jax.random.normal(own_key, dims, jnp.float32)
    if shards:
        drawn = drawn * level_of(own_key, dims, shards, -0.22, 0.18)
    return jnp.clip(drawn, -most, most).astype(held_as)


def gaussian_with(own_key, shape, width, limit, shards, heavy, kind=jnp.bfloat16):
    entries = width * jax.random.normal(own_key, shape, jnp.float32)
    if shards:
        entries = entries * level_of(own_key, shape, shards, -0.22, 0.18)
    return jnp.clip(spiked(entries, jax.random.fold_in(own_key, 3), *heavy), -limit, limit).astype(kind)


def setup_inputs(seed: int = 0) -> dict:
    seeds = jax.random.split(jax.random.key(seed), 15)
    return {
        "tokens": normal_values(seeds[0], (TOKENS, D), 1.0, 6.0, ((0, 32),)),
        "segments": draw_segments(jax.random.fold_in(seeds[14], 71), 0),
        "positions": draw_positions(jax.random.fold_in(seeds[14], 71), 0),
        "out_grad": gaussian_with(seeds[3], (TOKENS, D), 1.0, 6.0, ((0, 32),), (0, 1, 32, 2.75)),
        "ln1_gain": jnp.clip(1.0 + 0.1 * jax.random.normal(seeds[4], (D,), jnp.float32), 0.5, 1.5).astype(jnp.bfloat16),
        "ln1_bias": normal_values(seeds[5], (D,), 0.2, 1.0, ((0, 32),)),
        "qkv_weight": normal_values(seeds[6], (D, 3 * D), D ** -0.5, 0.125, ((0, 32),)),
        "qkv_bias": normal_values(seeds[7], (D, 3), 0.3, 1.5, ((0, 32),)),
        "o_weight": normal_values(seeds[8], (D, D), (D // 16) ** -0.5, 0.5, ((0, 32),)),
        "ln2_gain": jnp.clip(1.0 + 0.1 * jax.random.normal(seeds[9], (D,), jnp.float32), 0.5, 1.5).astype(jnp.bfloat16),
        "ln2_bias": normal_values(seeds[10], (D,), 0.2, 1.0, ((0, 32),)),
        "gate_weight": normal_values(seeds[11], (D, FF), D ** -0.5, 0.125, ((0, 32),)),
        "up_weight": normal_values(seeds[12], (D, FF), D ** -0.5, 0.125, ((0, 32),)),
        "down_weight": normal_values(seeds[13], (D, FF), FF ** -0.5, 0.078125, ((0, 32),)),
    }


highest = lax.Precision.HIGHEST

@jax.custom_vjp
def low(v):
    return lax.optimization_barrier(v.astype(jnp.bfloat16)).astype(jnp.float32)

@jax.custom_vjp
def low_back(v):
    return v

def low_keep(v):
    return (low(v), None)

def low_pass(kept, grad):
    return (grad,)

def back_keep(v):
    return (v, None)

def back_low(kept, grad):
    return (low(grad),)
low.defvjp(low_keep, low_pass)
low_back.defvjp(back_keep, back_low)

def layer_norm(values, gain_row, shift_row):
    mean_value = lax.optimization_barrier(jnp.mean(values, axis=-1, keepdims=True))
    centered = values - mean_value
    inv_std = lax.rsqrt(lax.optimization_barrier(jnp.mean(centered * centered, axis=-1, keepdims=True)) + 1e-05)
    return centered * inv_std * gain_row + shift_row

def half_turn(leading):
    middle = leading.shape[-1] // 2
    return jnp.concatenate([-leading[..., middle:], leading[..., :middle]], axis=-1)

def rotary(head_rows, position_ids):
    frequency = 10000.0 ** (-jnp.arange(0, ROT_DIMS, 2, dtype=jnp.float32) / ROT_DIMS)
    phases = position_ids.astype(jnp.float32)[:, None] * frequency[None, :]
    phases = jnp.concatenate([phases, phases], axis=1)
    cosine = jnp.cos(phases)[:, None, :]
    sine_rows = jnp.sin(phases)[:, None, :]
    leading = head_rows[..., :ROT_DIMS]
    turned = leading * cosine + half_turn(leading) * sine_rows
    return jnp.concatenate([turned, head_rows[..., ROT_DIMS:]], axis=-1)

def forward(params, inputs, segment_ids, position_ids):
    length = inputs.shape[0]
    act_one = low(layer_norm(inputs, params['ln1_gain'], params['ln1_bias']))
    bias_flat = jnp.transpose(params['qkv_bias']).reshape(-1)
    projected = low_back(jnp.dot(act_one, params['qkv_weight'], precision=highest) + bias_flat)
    query_heads = projected[:, :D].reshape(length, HEADS, HEAD_DIM)
    key_heads = projected[:, D:2 * D].reshape(length, HEADS, HEAD_DIM)
    value_heads = projected[:, 2 * D:].reshape(length, HEADS, HEAD_DIM)
    query_low = low(rotary(query_heads, position_ids))
    key_low = low(rotary(key_heads, position_ids))
    value_low = low(value_heads)
    index_row = jnp.arange(length)
    allowed = (index_row[None, :] <= index_row[:, None]) & (segment_ids[None, :] == segment_ids[:, None])
    scores = jnp.einsum('qhd,khd->hqk', query_low, key_low, precision=highest) * 0.125
    scores = low_back(jnp.where(allowed[None], scores, -1e+30))
    row_max = lax.optimization_barrier(jnp.max(scores, axis=-1, keepdims=True))
    weights = jnp.exp(scores - row_max)
    attn_probs = weights / lax.optimization_barrier(jnp.sum(weights, axis=-1, keepdims=True))
    mixed_out = jnp.einsum('hqk,khd->qhd', low(attn_probs), value_low, precision=highest).reshape(length, D)
    mixed_out = low(low_back(mixed_out))
    hidden = inputs + low_back(jnp.dot(mixed_out, params['o_weight'], precision=highest))
    act_two = low(layer_norm(hidden, params['ln2_gain'], params['ln2_bias']))
    gate_value = low_back(jnp.dot(act_two, params['gate_weight'], precision=highest))
    up_value = low_back(jnp.dot(act_two, params['up_weight'], precision=highest))
    middle = low(jax.nn.silu(gate_value) * up_value)
    return hidden + jnp.dot(middle, jnp.transpose(params['down_weight']), precision=highest)

def reference(tokens, segments, positions, out_grad, ln1_gain, ln1_bias, qkv_weight, qkv_bias, o_weight, ln2_gain, ln2_bias, gate_weight, up_weight, down_weight):
    params = {'ln1_gain': ln1_gain.astype(jnp.float32), 'ln1_bias': ln1_bias.astype(jnp.float32), 'qkv_weight': qkv_weight.astype(jnp.float32), 'qkv_bias': qkv_bias.astype(jnp.float32), 'o_weight': o_weight.astype(jnp.float32), 'ln2_gain': ln2_gain.astype(jnp.float32), 'ln2_bias': ln2_bias.astype(jnp.float32), 'gate_weight': gate_weight.astype(jnp.float32), 'up_weight': up_weight.astype(jnp.float32), 'down_weight': down_weight.astype(jnp.float32)}
    pack_count = TOKENS // SEQ
    pack_inputs = tokens.astype(jnp.float32).reshape(pack_count, SEQ, D)
    pack_grads = out_grad.astype(jnp.float32).reshape(pack_count, SEQ, D)
    pack_segments = segments.reshape(pack_count, SEQ)
    pack_positions = positions.reshape(pack_count, SEQ)

    def one_pack(running, item):
        inputs, segment_ids, position_ids, cotangent = item

        def layer_of(param_set, layer_in):
            return forward(param_set, layer_in, segment_ids, position_ids)
        result, pullback = jax.vjp(layer_of, params, inputs)
        param_grads, input_grads = pullback(cotangent)
        running = jax.tree.map(jnp.add, running, param_grads)
        return (running, (result.astype(jnp.bfloat16), input_grads.astype(jnp.bfloat16)))
    zeros = jax.tree.map(jnp.zeros_like, params)
    totals, (results, input_grads) = lax.scan(one_pack, zeros, (pack_inputs, pack_segments, pack_positions, pack_grads))
    return (results.reshape(TOKENS, D), input_grads.reshape(TOKENS, D), totals['ln1_gain'], totals['ln1_bias'], totals['qkv_weight'], totals['qkv_bias'], totals['o_weight'], totals['ln2_gain'], totals['ln2_bias'], totals['gate_weight'], totals['up_weight'], totals['down_weight'])
```

```python
import functools

import jax
import jax.numpy as jnp
from jax import lax
from jax.experimental import pallas as pl
from jax.experimental.pallas import tpu as pltpu
from jax.sharding import Mesh
from jax.sharding import PartitionSpec as P

HEAD_DIM = 64
ROT_DIMS = 16
PAIR = 2 * HEAD_DIM
PLANE = ("y", "x", "c")
ALL = ("g", "y", "x", "c")
bf16 = jnp.bfloat16
f32 = jnp.float32

epsilon = 1e-05
neg_large = -1e30
rope_base = 10000.0
score_scale = 0.125


def layer_stats(values):
    mean_value = jnp.mean(values, axis=-1, keepdims=True)
    centered = values - mean_value
    inv_std = lax.rsqrt(jnp.mean(centered * centered, axis=-1, keepdims=True) + epsilon)
    return (centered * inv_std, inv_std)


def norm_back(grad_rows, normed, inv_std, gain_row):
    scaled = grad_rows * gain_row
    inner = jnp.mean(scaled * normed, axis=-1, keepdims=True)
    return inv_std * (scaled - jnp.mean(scaled, axis=-1, keepdims=True) - normed * inner)


def contract(left, right, left_dim, right_dim, kind=f32):
    return lax.dot_general(
        left, right, (((left_dim,), (right_dim,)), ((), ())), preferred_element_type=f32
    ).astype(kind)


def swap(values, axis):
    return lax.ppermute(values, axis, [(0, 1), (1, 0)])


def plane_gather(rows):
    half = rows.shape[0] // 2
    over_x = swap(rows, "x")
    over_y = swap(rows, "y")
    corner_a = swap(over_y[:half], "x")
    corner_b = swap(over_x[half:], "y")
    pieces = []
    for chip in ((rows,), (over_x,), (over_y,), (corner_a, corner_b)):
        pieces += list(chip) + [swap(part, "c") for part in chip]
    return jnp.concatenate(pieces, axis=0)


def plane_reduce(slots):
    half = slots[0].shape[0] // 2
    chip = [
        slots[s].astype(f32) + swap(slots[s + 1], "c").astype(f32) for s in (0, 2, 4, 6)
    ]
    corner = chip[3].astype(bf16)
    from_x = swap(corner[:half], "x").astype(f32)
    from_y = swap(corner[half:], "y").astype(f32)
    to_x = jnp.concatenate([chip[1][:half], chip[1][half:] + from_y], axis=0)
    to_y = jnp.concatenate([chip[2][:half] + from_x, chip[2][half:]], axis=0)
    got_x = swap(to_x.astype(bf16), "x").astype(f32)
    got_y = swap(to_y.astype(bf16), "y").astype(f32)
    return chip[0] + got_x + got_y


def plane_exchange(slots):
    count = len(slots)
    return [slots[0]] + [
        lax.ppermute(slots[s], PLANE, [(i, i ^ s) for i in range(count)]) for s in range(1, count)
    ]


def plane_all_to_all(blocks):
    return lax.all_to_all(blocks, PLANE, 0, 0, tiled=True)


def turned(rows, cosine, sine, first):
    partner = jnp.where(first, pltpu.roll(rows, PAIR - ROT_DIMS // 2, 1), pltpu.roll(rows, ROT_DIMS // 2, 1))
    return rows * cosine + partner * sine


def lanes_of(rows):
    return lax.broadcasted_iota(jnp.int32, (rows, PAIR), 1)


def keep_head(values, head):
    lane = lanes_of(values.shape[0])
    inside = lane < HEAD_DIM if head == 0 else lane >= HEAD_DIM
    return jnp.where(inside, values, jnp.zeros_like(values))


def allowed_block(seg_col, seg_row, block, rows):
    same = seg_col[0, : (block + 1) * rows, :] == seg_row[0, :, block * rows : (block + 1) * rows]
    key_at = lax.broadcasted_iota(jnp.int32, same.shape, 0)
    query_at = lax.broadcasted_iota(jnp.int32, same.shape, 1) + block * rows
    return same & (key_at <= query_at)


def nt(left, right):
    return lax.dot_general(left, right, (((1,), (1,)), ((), ())), preferred_element_type=f32)


def tn(left, right):
    return lax.dot_general(left, right, (((0,), (0,)), ((), ())), preferred_element_type=f32)


def nn(left, right):
    return lax.dot_general(left, right, (((1,), (0,)), ((), ())), preferred_element_type=f32)


def attend_kernel(
    blocks, place, q_ref, k_ref, v_ref, bq_ref, bk_ref, bv_ref, cos_ref, sin_ref, col_ref, row_ref,
    mixed_ref, query_ref, key_ref, value_ref, total_ref,
):
    own = place[0]
    rows = q_ref.shape[2]
    first = lanes_of(rows) % HEAD_DIM < ROT_DIMS // 2
    for block in range(blocks):
        slot = jnp.bitwise_xor(own, block)
        span = slice(block * rows, (block + 1) * rows)
        cosine, sine = cos_ref[0, span, :], sin_ref[0, span, :]
        query_ref[0, span, :] = turned(q_ref[0, slot] + bq_ref[...], cosine, sine, first).astype(bf16)
        key_ref[0, span, :] = turned(k_ref[0, slot] + bk_ref[...], cosine, sine, first).astype(bf16)
        value_ref[0, span, :] = (v_ref[0, slot] + bv_ref[...]).astype(bf16)
    for block in range(blocks):
        slot = jnp.bitwise_xor(own, block)
        span = slice(block * rows, (block + 1) * rows)
        upto = (block + 1) * rows
        allowed = allowed_block(col_ref, row_ref, block, rows)
        mixed = jnp.zeros((PAIR, rows), f32)
        for head in range(2):
            query = keep_head(query_ref[0, span, :], head) * score_scale
            scores = jnp.where(allowed, nt(key_ref[0, :upto, :], query), neg_large)
            top = jnp.max(scores, axis=0, keepdims=True)
            weights = jnp.exp(scores - top)
            total = jnp.sum(weights, axis=0, keepdims=True)
            probs = (weights * (1.0 / total)).astype(bf16)
            mixed = mixed + tn(keep_head(value_ref[0, :upto, :], head), probs)
            total_ref[0, 0, head : head + 1, span] = top + jnp.log(total)
        mixed_ref[0, slot] = jnp.transpose(mixed).astype(bf16)


def attend_back_kernel(
    blocks, place, query_ref, key_ref, value_ref, grad_ref, total_ref, cos_ref, sin_ref, col_ref, row_ref,
    out_ref, dk_ref, dv_ref,
):
    own = place[0]
    pair = pl.program_id(1)
    rows = grad_ref.shape[2]
    width = out_ref.shape[3] // 3
    first = lanes_of(rows) % HEAD_DIM < ROT_DIMS // 2

    def put(slot, which, values):
        at = pl.multiple_of(which * width + pair * PAIR, PAIR)
        out_ref[0, slot, :, pl.ds(at, PAIR)] = values.astype(bf16)

    dk_ref[...] = jnp.zeros_like(dk_ref)
    dv_ref[...] = jnp.zeros_like(dv_ref)
    for block in range(blocks):
        slot = jnp.bitwise_xor(own, block)
        span = slice(block * rows, (block + 1) * rows)
        upto = (block + 1) * rows
        allowed = allowed_block(col_ref, row_ref, block, rows)
        dq = jnp.zeros((PAIR, rows), f32)
        for head in range(2):
            query = keep_head(query_ref[0, span, :], head) * score_scale
            grad = keep_head(grad_ref[0, slot], head)
            scores = jnp.where(allowed, nt(key_ref[0, :upto, :], query), neg_large)
            probs = jnp.exp(scores - total_ref[0, 0, head : head + 1, span])
            prob_grad = nt(value_ref[0, :upto, :], grad)
            inner = jnp.sum(probs * prob_grad, axis=0, keepdims=True)
            score_grad = (probs * (prob_grad - inner)).astype(bf16)
            dk_ref[:upto, :] += nn(score_grad, query)
            dv_ref[:upto, :] += nn(probs.astype(bf16), grad)
            dq = dq + tn(keep_head(key_ref[0, :upto, :], head), score_grad)
        put(slot, 0, turned(jnp.transpose(dq) * score_scale, cos_ref[0, span, :], -sin_ref[0, span, :], first))
    for block in range(blocks):
        slot = jnp.bitwise_xor(own, block)
        span = slice(block * rows, (block + 1) * rows)
        put(slot, 1, turned(dk_ref[span, :], cos_ref[0, span, :], -sin_ref[0, span, :], first))
        put(slot, 2, dv_ref[span, :])


def attention(place, projected, bias, cosine, sine, seg_col, seg_row):
    packs, blocks, rows, width = projected.shape
    width //= 3
    pairs, seq = width // PAIR, blocks * rows

    def part(which):
        return pl.BlockSpec((1, blocks, rows, PAIR), lambda p, h, place: (p, 0, 0, which * pairs + h))

    def part_bias(which):
        return pl.BlockSpec((1, PAIR), lambda p, h, place: (0, which * pairs + h))

    def at_pack(*shape):
        return pl.BlockSpec((1, *shape), lambda p, h, place: (jnp.bitwise_xor(p, place[1]), 0, 0))

    kept = pl.BlockSpec((1, seq, PAIR), lambda p, h, place: (p, 0, h))
    return pl.pallas_call(
        functools.partial(attend_kernel, blocks),
        grid_spec=pltpu.PrefetchScalarGridSpec(
            num_scalar_prefetch=1,
            grid=(packs, pairs),
            in_specs=[part(0), part(1), part(2), part_bias(0), part_bias(1), part_bias(2),
                      at_pack(seq, PAIR), at_pack(seq, PAIR), at_pack(seq, 1), at_pack(1, seq)],
            out_specs=[
                pl.BlockSpec((1, blocks, rows, PAIR), lambda p, h, place: (p, 0, 0, h)),
                kept, kept, kept,
                pl.BlockSpec((1, 1, 2, seq), lambda p, h, place: (p, h, 0, 0)),
            ],
        ),
        out_shape=[
            jax.ShapeDtypeStruct((packs, blocks, rows, width), bf16),
            *[jax.ShapeDtypeStruct((packs, seq, width), bf16)] * 3,
            jax.ShapeDtypeStruct((packs, pairs, 2, seq), f32),
        ],
        compiler_params=pltpu.CompilerParams(vmem_limit_bytes=48 * 1024 * 1024),
        cost_estimate=pl.CostEstimate(
            flops=packs * seq * seq * width * 4, bytes_accessed=packs * seq * width * 24,
            transcendentals=packs * seq * seq * pairs,
        ),
    )(place, projected, projected, projected, bias, bias, bias, cosine, sine, seg_col, seg_row)


def attention_back(place, query, key, value, grad, totals, cosine, sine, seg_col, seg_row):
    packs, blocks, rows, width = grad.shape
    pairs, seq = width // PAIR, blocks * rows

    def at_pack(*shape):
        return pl.BlockSpec((1, *shape), lambda p, h, place: (jnp.bitwise_xor(p, place[1]), 0, 0))

    kept = pl.BlockSpec((1, seq, PAIR), lambda p, h, place: (p, 0, h))
    return pl.pallas_call(
        functools.partial(attend_back_kernel, blocks),
        grid_spec=pltpu.PrefetchScalarGridSpec(
            num_scalar_prefetch=1,
            grid=(packs, pairs),
            in_specs=[
                kept, kept, kept,
                pl.BlockSpec((1, blocks, rows, PAIR), lambda p, h, place: (p, 0, 0, h)),
                pl.BlockSpec((1, 1, 2, seq), lambda p, h, place: (p, h, 0, 0)),
                at_pack(seq, PAIR), at_pack(seq, PAIR), at_pack(seq, 1), at_pack(1, seq),
            ],
            out_specs=pl.BlockSpec((1, blocks, rows, 3 * width), lambda p, h, place: (p, 0, 0, 0)),
            scratch_shapes=[pltpu.VMEM((seq, PAIR), f32), pltpu.VMEM((seq, PAIR), f32)],
        ),
        out_shape=jax.ShapeDtypeStruct((packs, blocks, rows, 3 * width), bf16),
        compiler_params=pltpu.CompilerParams(vmem_limit_bytes=48 * 1024 * 1024),
        cost_estimate=pl.CostEstimate(
            flops=packs * seq * seq * width * 10, bytes_accessed=packs * seq * width * 16,
            transcendentals=packs * seq * seq * pairs,
        ),
    )(place, query, key, value, grad, totals, cosine, sine, seg_col, seg_row)


def local(
    tokens, segments, positions, out_grad, ln1_gain, ln1_bias, qkv_weight, qkv_bias, o_weight,
    ln2_gain, ln2_bias, gate_weight, up_weight, down_weight,
):
    rows, width = tokens.shape
    shard = qkv_weight.shape[0]
    ffn = gate_weight.shape[1]
    heads = width // HEAD_DIM
    team = lax.axis_size(PLANE)
    depth = lax.axis_size("g")
    devices = team * depth
    packs = lax.axis_size("y")
    blocks = team // packs
    seq = blocks * rows
    my_heads = heads // team
    my_width = my_heads * HEAD_DIM
    my_ffn = ffn // team
    pad_ffn = -(-my_ffn // 128) * 128
    me = lax.axis_index(PLANE)
    own_block = lax.axis_index("x") * 2 + lax.axis_index("c")
    place = jnp.stack([own_block, lax.axis_index("y")]).astype(jnp.int32)
    aligned = shard == HEAD_DIM

    vectors = jnp.stack([ln1_gain, ln1_bias, ln2_gain, ln2_bias], axis=0)
    vectors = jnp.concatenate([vectors, jnp.transpose(qkv_bias)], axis=0).astype(f32).reshape(-1)
    small = jnp.concatenate([vectors, segments.astype(f32), positions.astype(f32)])
    small = lax.all_to_all(
        jnp.broadcast_to(small[None], (devices, small.shape[0])), ALL, 0, 0, tiled=True
    )
    vectors = jnp.transpose(small[:, : 7 * shard].reshape(devices, 7, shard), (1, 0, 2)).reshape(7, width)
    gain_one, shift_one, gain_two, shift_two = (vectors[i][None, :] for i in range(4))
    my_plane = lax.dynamic_slice_in_dim(small[:, 7 * shard :], lax.axis_index("g") * team, team, 0)
    segment_all = my_plane[:, :rows].reshape(packs, seq)
    position_all = my_plane[:, rows:].reshape(packs, seq)
    bias_mine = lax.dynamic_slice_in_dim(
        vectors[4:7].reshape(3, my_heads, team, HEAD_DIM), me, 1, 2
    ).reshape(1, 3 * my_width)

    qkv_send = jnp.transpose(
        qkv_weight.reshape(shard, 3 * my_heads, team, HEAD_DIM), (2, 0, 1, 3)
    ).reshape(team, shard, 3 * my_width)
    qkv_mine = plane_all_to_all(qkv_send).reshape(team * shard, 3 * my_width)

    def ffn_columns(weight):
        split = jnp.transpose(weight.reshape(shard, team, my_ffn), (1, 0, 2))
        return jnp.pad(split, ((0, 0), (0, 0), (0, pad_ffn - my_ffn)))

    ffn_send = jnp.concatenate(
        [ffn_columns(gate_weight), ffn_columns(up_weight), ffn_columns(down_weight)], axis=2
    )
    ffn_mine = plane_all_to_all(ffn_send).reshape(team * shard, 3 * pad_ffn)

    def over_g(piece):
        return lax.all_gather(piece, "g", axis=0, tiled=True)

    if aligned:
        out_rows = over_g(o_weight)
        out_full = plane_gather(out_rows)
    else:
        out_abs = lax.all_gather(o_weight, ALL, axis=0, tiled=True)
        out_abs = out_abs.reshape(my_heads, team, HEAD_DIM, width)
        out_full = jnp.concatenate(
            [jnp.take(out_abs, jnp.bitwise_xor(me, s), axis=1).reshape(my_width, width) for s in range(team)],
            axis=0,
        )
    qkv_full = over_g(qkv_mine)
    gate_up_full = over_g(ffn_mine[:, : 2 * pad_ffn])
    down_full = over_g(ffn_mine[:, 2 * pad_ffn :])

    inputs = tokens.astype(f32)
    normed_one, inv_one = layer_stats(inputs)
    act_one = plane_gather((normed_one * gain_one + shift_one).astype(bf16))
    projected = contract(act_one, qkv_full, 1, 0)
    frequency = rope_base ** (-jnp.arange(0, ROT_DIMS, 2, dtype=f32) / ROT_DIMS)
    within = jnp.arange(PAIR) % HEAD_DIM
    phases = position_all[:, :, None] * jnp.where(within < ROT_DIMS, frequency[within % (ROT_DIMS // 2)], 0.0)
    cosine = jnp.cos(phases)
    sine = jnp.sin(phases) * jnp.where(within < ROT_DIMS // 2, -1.0, 1.0)
    seg_col, seg_row = segment_all[:, :, None], segment_all[:, None, :]
    mixed, query, key, value, totals = attention(
        place, projected.reshape(packs, blocks, rows, 3 * my_width), bias_mine, cosine, sine, seg_col, seg_row
    )
    mixed = mixed.reshape(team, rows, my_width)
    mixed_own = jnp.concatenate(plane_exchange([mixed[s] for s in range(team)]), axis=1)
    hidden = inputs + contract(mixed_own, out_full, 1, 0)

    normed_two, inv_two = layer_stats(hidden)
    act_two = plane_gather((normed_two * gain_two + shift_two).astype(bf16))
    cotangent = plane_gather(out_grad)
    gate_up = contract(act_two, gate_up_full, 1, 0)
    gate_value, up_value = gate_up[:, :pad_ffn], gate_up[:, pad_ffn:]
    gate_sigmoid = jax.nn.sigmoid(gate_value)
    gate_silu = gate_value * gate_sigmoid
    middle_low = (gate_silu * up_value).astype(bf16)

    def slots_of(left, right):
        return [
            contract(left[s * rows : (s + 1) * rows], right, 1, 1, bf16) for s in range(team)
        ]

    output = (hidden + plane_reduce(slots_of(middle_low, down_full))).astype(bf16)

    middle_grad = contract(cotangent, down_full, 1, 0)
    gate_grad = middle_grad * up_value * (gate_sigmoid * (1.0 + gate_value * (1.0 - gate_sigmoid)))
    gate_up_grad = jnp.concatenate([gate_grad.astype(bf16), (middle_grad * gate_silu).astype(bf16)], axis=1)
    norm_grad_two = plane_reduce(slots_of(gate_up_grad, gate_up_full))
    hidden_grad = out_grad.astype(f32) + norm_back(norm_grad_two, normed_two, inv_two, gain_two)
    hidden_low = hidden_grad.astype(bf16)

    def own_rows(grad_sum):
        return lax.psum_scatter(grad_sum, "g", scatter_dimension=0, tiled=True)

    def back_to_rows(columns):
        return plane_all_to_all(columns.reshape(team, shard, columns.shape[1]))

    def ffn_rows(received, which):
        part = received[:, :, which * pad_ffn : which * pad_ffn + my_ffn].astype(f32)
        return jnp.transpose(part, (1, 0, 2)).reshape(shard, ffn)

    down_share = back_to_rows(own_rows(contract(cotangent, middle_low, 0, 0, bf16)))
    gate_up_share = back_to_rows(own_rows(contract(act_two, gate_up_grad, 0, 0, bf16)))

    mixed_grad = contract(hidden_low, out_full, 1, 1, bf16)
    mixed_grad = plane_exchange([mixed_grad[:, s * my_width : (s + 1) * my_width] for s in range(team)])
    mixed_grad = jnp.stack(mixed_grad).reshape(packs, blocks, rows, my_width)
    hidden_all = plane_gather(hidden_low)
    out_sum = contract(mixed.reshape(team * rows, my_width), hidden_all, 0, 0, bf16)
    if aligned:
        out_share = own_rows(out_sum).astype(f32)
    else:
        spread = jnp.zeros((my_heads, team, HEAD_DIM, width), bf16)
        spread = lax.dynamic_update_slice_in_dim(
            spread, out_sum.reshape(my_heads, 1, HEAD_DIM, width), me, 1
        )
        out_share = lax.psum_scatter(
            spread.reshape(width, width).astype(f32), ALL, scatter_dimension=0, tiled=True
        )
    qkv_grad = attention_back(
        place, query, key, value, mixed_grad, totals, cosine, sine, seg_col, seg_row
    ).reshape(team * rows, 3 * my_width)
    norm_grad_one = plane_reduce(slots_of(qkv_grad, qkv_full))
    input_grad = (hidden_grad + norm_back(norm_grad_one, normed_one, inv_one, gain_one)).astype(bf16)
    qkv_share = back_to_rows(own_rows(contract(act_one, qkv_grad, 0, 0, bf16)))
    qkv_share = jnp.transpose(
        qkv_share.reshape(team, shard, 3 * my_heads, HEAD_DIM), (1, 2, 0, 3)
    ).reshape(shard, 3 * width).astype(f32)

    bias_sum = jnp.sum(qkv_grad.astype(f32), axis=0).reshape(3, my_heads, 1, HEAD_DIM)
    mine = (jnp.arange(team) == me).astype(f32)[None, None, :, None]
    terms = jnp.concatenate(
        [
            jnp.sum(norm_grad_one * normed_one, axis=0)[None],
            jnp.sum(norm_grad_one, axis=0)[None],
            (bias_sum * mine).reshape(3, width),
            jnp.sum(norm_grad_two * normed_two, axis=0)[None],
            jnp.sum(norm_grad_two, axis=0)[None],
        ],
        axis=0,
    )
    terms = jnp.transpose(terms.reshape(7, devices, shard), (1, 0, 2)).reshape(devices, 7 * shard)
    vector_share = jnp.sum(lax.all_to_all(terms, ALL, 0, 0, tiled=True), axis=0).reshape(7, shard)
    return (
        output,
        input_grad,
        vector_share[0],
        vector_share[1],
        qkv_share,
        jnp.transpose(vector_share[2:5]),
        out_share,
        vector_share[5],
        vector_share[6],
        ffn_rows(gate_up_share, 0),
        ffn_rows(gate_up_share, 1),
        ffn_rows(down_share, 0),
    )


def solution(mesh):
    dp, ctx = mesh.shape["dp"], mesh.shape["ctx"]
    split = Mesh(mesh.devices.reshape(dp // 2, 2, ctx // 2, 2), ALL)
    row, flat = P(ALL, None), P(ALL)
    return jax.shard_map(
        local,
        mesh=split,
        in_specs=(row, flat, flat, row, flat, flat, row, row, row, flat, flat, row, row, row),
        out_specs=(row, row, flat, flat, row, row, row, flat, flat, row, row, row),
        check_vma=False,
    )
```

```python
import functools

import jax
import jax.numpy as jnp
from jax import lax
from jax.experimental import pallas as pl
from jax.experimental.pallas import tpu as pltpu
from jax.sharding import Mesh
from jax.sharding import PartitionSpec as P

HEAD_DIM = 64
ROT_DIMS = 16
PAIR = 2 * HEAD_DIM
PLANE = ("y", "x", "c")
ALL = ("g", "y", "x", "c")
bf16 = jnp.bfloat16
f32 = jnp.float32

epsilon = 1e-05
neg_large = -1e30
rope_base = 10000.0
score_scale = 0.125


def layer_stats(values):
    mean_value = jnp.mean(values, axis=-1, keepdims=True)
    centered = values - mean_value
    inv_std = lax.rsqrt(jnp.mean(centered * centered, axis=-1, keepdims=True) + epsilon)
    return (centered * inv_std, inv_std)


def norm_back(grad_rows, normed, inv_std, gain_row):
    scaled = grad_rows * gain_row
    inner = jnp.mean(scaled * normed, axis=-1, keepdims=True)
    return inv_std * (scaled - jnp.mean(scaled, axis=-1, keepdims=True) - normed * inner)


def contract(left, right, left_dim, right_dim, kind=f32):
    return lax.dot_general(
        left, right, (((left_dim,), (right_dim,)), ((), ())), preferred_element_type=f32
    ).astype(kind)


def after(values, *others):
    return lax.optimization_barrier((values, *others))[0]


def fenced(function, *operands):
    shapes = jax.eval_shape(function, *operands)
    return lax.cond(
        lax.axis_index("g") < lax.axis_size("g"),
        function,
        lambda *_: jax.tree.map(lambda leaf: jnp.zeros(leaf.shape, leaf.dtype), shapes),
        *operands,
    )


def swap(values, axis):
    return lax.ppermute(values, axis, [(0, 1), (1, 0)])


def join_kernel(*refs):
    *piece_refs, out_ref = refs
    at = 0
    for piece in piece_refs:
        out_ref[at : at + piece.shape[0], :] = piece[...]
        at += piece.shape[0]


def join(pieces, lead=0):
    rows, width = sum(piece.shape[0] for piece in pieces), pieces[0].shape[1]
    return pl.pallas_call(
        join_kernel,
        grid=(4,),
        in_specs=[pl.BlockSpec((piece.shape[0], width // 4), lambda i: (0, i)) for piece in pieces],
        out_specs=pl.BlockSpec((rows, width // 4), lambda i: (0, i)),
        out_shape=jax.ShapeDtypeStruct((rows, width), pieces[0].dtype),
        **limits(lead),
    )(*pieces)


def chip_pieces(rows, *first):
    half = rows.shape[0] // 2
    over_x = swap(rows, "x")
    over_y = swap(rows, "y")
    if first:
        over_x, over_y = lax.optimization_barrier((over_x, over_y, *first))[:2]
    return [rows, over_x, over_y, swap(over_y[:half], "x"), swap(over_x[half:], "y")]


def halves_of(pieces, *first, lead=0):
    if first:
        pieces = lax.optimization_barrier((*pieces, *first))[: len(pieces)]
    mine = join(pieces, lead)
    return mine, swap(mine, "c")


def send_kernel(left_ref, right_ref, out_ref):
    out_ref[...] = nt(left_ref[...], right_ref[...]).astype(bf16)


def keep_kernel(left_ref, right_ref, other_ref, corner_ref, x_ref, y_ref, own_ref):
    s = pl.program_id(0)
    total = nt(left_ref[...], right_ref[...]) + other_ref[...].astype(f32)

    @pl.when(s == 0)
    def _():
        corner_ref[...] = total.astype(bf16)

    for which, ref in ((1, x_ref), (2, y_ref), (3, own_ref)):

        @pl.when(s == which)
        def _(ref=ref):
            ref[...] = total.astype(ref.dtype)


def corner_first(s):
    return jnp.where(s == 0, 3, jnp.where(s == 3, 0, s))


def plane_send(left, right, at, lead=0):
    rows, depth, width = left.shape[0] // 8, left.shape[1], right.shape[0]
    terms = pl.pallas_call(
        send_kernel,
        grid=(2,),
        in_specs=[
            pl.BlockSpec((2 * rows, depth), lambda s: (s + 2, 0)),
            pl.BlockSpec((width, depth), lambda s: (0, at)),
        ],
        out_specs=pl.BlockSpec((2 * rows, width), lambda s: (s, 0)),
        out_shape=jax.ShapeDtypeStruct((4 * rows, width), bf16),
        **limits(lead),
    )(left, right)
    return swap(terms, "c")


def plane_keep(left, right, at, other, kind=f32, lead=0):
    rows, depth, width = left.shape[0] // 8, left.shape[1], right.shape[0]
    whole = pl.BlockSpec((rows, width), lambda s: (0, 0))
    return pl.pallas_call(
        keep_kernel,
        grid=(4,),
        in_specs=[
            pl.BlockSpec((rows, depth), lambda s: (corner_first(s), 0)),
            pl.BlockSpec((width, depth), lambda s: (0, at)),
            pl.BlockSpec((rows, width), lambda s: (corner_first(s), 0)),
        ],
        out_specs=[whole] * 4,
        out_shape=[jax.ShapeDtypeStruct((rows, width), kind) for kind in (bf16, kind, kind, f32)],
        **limits(lead),
    )(left, right, other)


def plane_direct(kept):
    corner, for_x, for_y, own = kept
    far = lax.ppermute(corner, ("y", "x"), [(0, 3), (1, 2), (2, 1), (3, 0)])
    return own, swap(for_x, "x"), swap(for_y, "y"), far


def plane_corner(kept):
    corner, for_x, for_y, own = kept
    half = corner.shape[0] // 2
    from_x = swap(corner[:half], "x")
    from_y = swap(corner[half:], "y")
    to_x = jnp.concatenate([for_x[:half], for_x[half:] + from_y.astype(f32)], axis=0).astype(bf16)
    to_y = jnp.concatenate([for_y[:half] + from_x.astype(f32), for_y[half:]], axis=0).astype(bf16)
    return own, to_x, to_y


def plane_neighbours(terms):
    own, to_x, to_y = terms
    return own, swap(to_x, "x"), swap(to_y, "y")


def total_of(terms):
    return sum(term.astype(f32) for term in terms[1:]) + terms[0]


def sum_kernel(count, *refs):
    *in_refs, out_ref = refs
    total = tn(in_refs[0][...], in_refs[count][...])
    for left_ref, right_ref in zip(in_refs[1:count], in_refs[count + 1 :]):
        total += tn(left_ref[...], right_ref[...])
    out_ref[...] = total.astype(bf16)


def row_sum(left, right, lead=0):
    width, columns = left[0].shape[1], right[0].shape[1]
    step = min(width, 512)
    rows = sum(piece.shape[0] for piece in left)
    return pl.pallas_call(
        functools.partial(sum_kernel, len(left)),
        grid=(width // step,),
        in_specs=[
            *[pl.BlockSpec((piece.shape[0], step), lambda i: (0, i)) for piece in left],
            *[pl.BlockSpec(piece.shape, lambda i: (0, 0)) for piece in right],
        ],
        out_specs=pl.BlockSpec((step, columns), lambda i: (i, 0)),
        out_shape=jax.ShapeDtypeStruct((width, columns), bf16),
        **limits(lead),
    )(*left, *right)


def deep_reduce(blocks):
    depth = lax.axis_index("g")
    slots = [lax.dynamic_index_in_dim(blocks, jnp.bitwise_xor(depth, j), 0, False) for j in range(4)]
    ends = lax.ppermute(slots[3], "g", [(0, 1), (3, 2)])
    middle = lax.ppermute(slots[3], "g", [(1, 2), (2, 1)])
    near = lax.ppermute(slots[1], "g", [(0, 1), (1, 0), (2, 3), (3, 2)])
    far = lax.ppermute(
        (slots[2].astype(f32) + ends.astype(f32)).astype(bf16), "g", [(0, 2), (1, 3), (2, 0), (3, 1)]
    )
    return slots[0].astype(f32) + middle.astype(f32) + near.astype(f32) + far.astype(f32)


def plane_all_to_all(blocks):
    return lax.all_to_all(blocks, PLANE, 0, 0, tiled=True)


def turned(rows, cosine, sine, first):
    partner = jnp.where(first, pltpu.roll(rows, PAIR - ROT_DIMS // 2, 1), pltpu.roll(rows, ROT_DIMS // 2, 1))
    return rows * cosine + partner * sine


def lanes_of(rows):
    return lax.broadcasted_iota(jnp.int32, (rows, PAIR), 1)


def keep_head(values, head):
    lane = lanes_of(values.shape[0])
    inside = lane < HEAD_DIM if head == 0 else lane >= HEAD_DIM
    return jnp.where(inside, values, jnp.zeros_like(values))


def allowed_block(seg_col, seg_row, block, rows):
    same = seg_col[0, : (block + 1) * rows, :] == seg_row[0, :, block * rows : (block + 1) * rows]
    key_at = lax.broadcasted_iota(jnp.int32, same.shape, 0)
    query_at = lax.broadcasted_iota(jnp.int32, same.shape, 1) + block * rows
    return same & (key_at <= query_at)


def where_is(place, block):
    return jnp.bitwise_xor(place[1], block % 2), jnp.bitwise_xor(place[0], block // 2)


def nt(left, right):
    return lax.dot_general(left, right, (((1,), (1,)), ((), ())), preferred_element_type=f32)


def tn(left, right):
    return lax.dot_general(left, right, (((0,), (0,)), ((), ())), preferred_element_type=f32)


def nn(left, right):
    return lax.dot_general(left, right, (((1,), (0,)), ((), ())), preferred_element_type=f32)


def attend_kernel(
    blocks, place, query_ref, key_ref, value_ref, col_ref, row_ref, mixed_ref, halves_ref, total_ref,
):
    rows = mixed_ref.shape[2]
    for block in range(blocks):
        span = slice(block * rows, (block + 1) * rows)
        upto = (block + 1) * rows
        allowed = allowed_block(col_ref, row_ref, block, rows)
        mixed = jnp.zeros((PAIR, rows), f32)
        for head in range(2):
            query = keep_head(query_ref[0, span, :], head) * score_scale
            scores = jnp.where(allowed, nt(key_ref[0, :upto, :], query), neg_large)
            top = jnp.max(scores, axis=0, keepdims=True)
            weights = jnp.exp(scores - top)
            total = jnp.sum(weights, axis=0, keepdims=True)
            probs = (weights * (1.0 / total)).astype(bf16)
            mixed = mixed + tn(keep_head(value_ref[0, :upto, :], head), probs)
            total_ref[0, 0, head : head + 1, span] = top + jnp.log(total)
        mixed = jnp.transpose(mixed).astype(bf16)
        mixed_ref[0, block] = mixed
        half, entry = where_is(place, block)
        halves_ref[half, 0, entry] = mixed


def attend_back_kernel(
    blocks, place, query_ref, key_ref, value_ref, grad_ref, total_ref, cos_ref, sin_ref, col_ref, row_ref,
    out_ref, dk_ref, dv_ref,
):
    pair = pl.program_id(1)
    rows = grad_ref.shape[2]
    width = out_ref.shape[4] // 3
    first = lanes_of(rows) % HEAD_DIM < ROT_DIMS // 2

    def put(block, which, values):
        half, entry = where_is(place, block)
        at = pl.multiple_of(which * width + pair * PAIR, PAIR)
        out_ref[half, 0, entry, :, pl.ds(at, PAIR)] = values.astype(bf16)

    dk_ref[...] = jnp.zeros_like(dk_ref)
    dv_ref[...] = jnp.zeros_like(dv_ref)
    for block in range(blocks):
        span = slice(block * rows, (block + 1) * rows)
        upto = (block + 1) * rows
        allowed = allowed_block(col_ref, row_ref, block, rows)
        dq = jnp.zeros((PAIR, rows), f32)
        for head in range(2):
            query = keep_head(query_ref[0, span, :], head) * score_scale
            grad = keep_head(grad_ref[0, block], head)
            scores = jnp.where(allowed, nt(key_ref[0, :upto, :], query), neg_large)
            probs = jnp.exp(scores - total_ref[0, 0, head : head + 1, span])
            prob_grad = nt(value_ref[0, :upto, :], grad)
            inner = jnp.sum(probs * prob_grad, axis=0, keepdims=True)
            score_grad = (probs * (prob_grad - inner)).astype(bf16)
            dk_ref[:upto, :] += nn(score_grad, query)
            dv_ref[:upto, :] += nn(probs.astype(bf16), grad)
            dq = dq + tn(keep_head(key_ref[0, :upto, :], head), score_grad)
        put(block, 0, turned(jnp.transpose(dq) * score_scale, cos_ref[0, span, :], -sin_ref[0, span, :], first))
    for block in range(blocks):
        span = slice(block * rows, (block + 1) * rows)
        put(block, 1, turned(dk_ref[span, :], cos_ref[0, span, :], -sin_ref[0, span, :], first))
        put(block, 2, dv_ref[span, :])


def limits(lead=0):
    return dict(
        compiler_params=pltpu.CompilerParams(vmem_limit_bytes=56 * 1024 * 1024),
        cost_estimate=pl.CostEstimate(flops=lead * 10**9, bytes_accessed=lead * 3 * 10**6, transcendentals=0),
    )


def qkv_parts(seq, pairs):
    return [
        pl.BlockSpec((1, seq, PAIR), lambda p, h, place, which=which: (p, 0, which * pairs + h))
        for which in range(3)
    ]


def at_pack(*shape):
    rest = (0,) * len(shape)
    return pl.BlockSpec((1, *shape), lambda p, h, place: (jnp.bitwise_xor(p, place[2]), *rest))


def attention(place, qkv, blocks, seg_col, seg_row, lead=0):
    packs, seq, width = qkv.shape
    width //= 3
    rows, pairs = seq // blocks, width // PAIR
    return pl.pallas_call(
        functools.partial(attend_kernel, blocks),
        grid_spec=pltpu.PrefetchScalarGridSpec(
            num_scalar_prefetch=1,
            grid=(packs, pairs),
            in_specs=[*qkv_parts(seq, pairs), at_pack(seq, 1), at_pack(1, seq)],
            out_specs=[
                pl.BlockSpec(
                    (1, blocks, rows, PAIR), lambda p, h, place: (jnp.bitwise_xor(p, place[2]), 0, 0, h)
                ),
                pl.BlockSpec((2, 1, 2, rows, PAIR), lambda p, h, place: (0, p, 0, 0, h)),
                pl.BlockSpec((1, 1, 2, seq), lambda p, h, place: (p, h, 0, 0)),
            ],
        ),
        out_shape=[
            jax.ShapeDtypeStruct((packs, blocks, rows, width), bf16),
            jax.ShapeDtypeStruct((2, packs, 2, rows, width), bf16),
            jax.ShapeDtypeStruct((packs, pairs, 2, seq), f32),
        ],
        **limits(lead),
    )(place, qkv, qkv, qkv, seg_col, seg_row)


def attention_back(place, qkv, grad, totals, cosine, sine, seg_col, seg_row, lead=0):
    packs, blocks, rows, width = grad.shape
    pairs, seq = width // PAIR, blocks * rows
    return pl.pallas_call(
        functools.partial(attend_back_kernel, blocks),
        grid_spec=pltpu.PrefetchScalarGridSpec(
            num_scalar_prefetch=1,
            grid=(packs, pairs),
            in_specs=[
                *qkv_parts(seq, pairs),
                pl.BlockSpec(
                    (1, blocks, rows, PAIR), lambda p, h, place: (jnp.bitwise_xor(p, place[2]), 0, 0, h)
                ),
                pl.BlockSpec((1, 1, 2, seq), lambda p, h, place: (p, h, 0, 0)),
                at_pack(seq, PAIR), at_pack(seq, PAIR), at_pack(seq, 1), at_pack(1, seq),
            ],
            out_specs=pl.BlockSpec((2, 1, 2, rows, 3 * width), lambda p, h, place: (0, p, 0, 0, 0)),
            scratch_shapes=[pltpu.VMEM((seq, PAIR), f32)] * 2,
        ),
        out_shape=jax.ShapeDtypeStruct((2, packs, 2, rows, 3 * width), bf16),
        **limits(lead),
    )(place, qkv, qkv, qkv, grad, totals, cosine, sine, seg_col, seg_row)


def norm_kernel(*refs):
    *piece_refs, gain_ref, shift_ref, act_ref = refs
    step, at = 64, 0
    for piece in piece_refs:
        for row in range(0, piece.shape[0], step):
            normed = layer_stats(piece[row : row + step, :].astype(f32))[0]
            act_ref[at : at + step, :] = (normed * gain_ref[...] + shift_ref[...]).astype(bf16)
            at += step


def norm_rows(pieces, gain, shift, lead=0):
    count, width = sum(piece.shape[0] for piece in pieces), gain.shape[1]
    return pl.pallas_call(
        norm_kernel,
        out_shape=jax.ShapeDtypeStruct((count, width), bf16),
        **limits(lead),
    )(*pieces, gain, shift)


def pick(halves, steps):
    return jnp.where(pl.program_id(0) < steps // 2, halves[0][...], halves[1][...])


def project_kernel(place, act0_ref, act1_ref, weight_ref, bias_ref, cos_ref, sin_ref, out_ref, act_ref):
    act = pick((act0_ref, act1_ref), 8)
    act_ref[...] = act
    projected = nn(act, weight_ref[...]) + bias_ref[...]
    rows, width = projected.shape
    first = lanes_of(rows) % HEAD_DIM < ROT_DIMS // 2
    cosine, sine = cos_ref[0], sin_ref[0]
    for at in range(0, width, PAIR):
        part = projected[:, at : at + PAIR]
        if at < 2 * width // 3:
            part = turned(part, cosine, sine, first)
        out_ref[0, :, at : at + PAIR] = part.astype(bf16)


def project(place, act, weight, bias, cosine, sine, lead=0):
    count, depth = act[0].shape
    width = weight.shape[1]
    packs, seq, _ = cosine.shape
    rows = count // 4

    def block_of(s, place):
        return jnp.bitwise_xor(place[0], s % 2) * 2 + jnp.bitwise_xor(place[1], s // 4)

    def table(s, place):
        return (jnp.bitwise_xor(place[2], s // 2 % 2), block_of(s, place), 0)

    return pl.pallas_call(
        project_kernel,
        grid_spec=pltpu.PrefetchScalarGridSpec(
            num_scalar_prefetch=1,
            grid=(8,),
            in_specs=[
                *half_specs(rows, depth),
                pl.BlockSpec((depth, width), lambda s, place: (0, 0)),
                pl.BlockSpec((1, width), lambda s, place: (0, 0)),
                pl.BlockSpec((1, rows, PAIR), table),
                pl.BlockSpec((1, rows, PAIR), table),
            ],
            out_specs=[
                pl.BlockSpec((1, rows, width), lambda s, place: (s // 2 % 2, block_of(s, place), 0)),
                pl.BlockSpec((rows, depth), lambda s, place: (s, 0)),
            ],
        ),
        out_shape=[
            jax.ShapeDtypeStruct((packs, seq, width), bf16), jax.ShapeDtypeStruct((2 * count, depth), bf16)
        ],
        **limits(lead),
    )(place, *act, weight, bias, cosine, sine)


def slot_of(s, place):
    return jnp.bitwise_xor(place[3], s // 4 + (s // 2 % 2) * 4 + (s % 2) * 2)


def half_specs(rows, width, steps=8):
    half = steps // 2
    return [
        pl.BlockSpec((rows, width), lambda s, *place: (jnp.minimum(s, half - 1), 0)),
        pl.BlockSpec((rows, width), lambda s, *place: (jnp.maximum(s - half, 0), 0)),
    ]


def out_kernel(place, mixed_ref, w0_ref, w1_ref, token_ref, gain_ref, shift_ref, hidden_ref, act_ref, sum_ref):
    s = pl.program_id(0)

    @pl.when(s == 0)
    def _():
        sum_ref[...] = token_ref[...].astype(f32)

    @pl.when(s < 4)
    def _():
        sum_ref[...] += nn(mixed_ref[0], w0_ref[...])

    @pl.when(s >= 4)
    def _():
        sum_ref[...] += nn(mixed_ref[0], w1_ref[...])

    @pl.when(s == 7)
    def _():
        hidden = sum_ref[...]
        hidden_ref[...] = hidden
        act_ref[...] = (layer_stats(hidden)[0] * gain_ref[...] + shift_ref[...]).astype(bf16)


def out_rows_of(place, mixed, weight, tokens, gain, shift, lead=0):
    rows, width = tokens.shape
    part = mixed.shape[2]
    whole = pl.BlockSpec((rows, width), lambda s, place: (0, 0))
    vector = pl.BlockSpec((1, width), lambda s, place: (0, 0))
    return pl.pallas_call(
        out_kernel,
        grid_spec=pltpu.PrefetchScalarGridSpec(
            num_scalar_prefetch=1,
            grid=(8,),
            in_specs=[
                pl.BlockSpec((1, rows, part), lambda s, place: (slot_of(s, place), 0, 0)),
                *half_specs(part, width), whole, vector, vector,
            ],
            out_specs=[whole, whole],
            scratch_shapes=[pltpu.VMEM((rows, width), f32)],
        ),
        out_shape=[jax.ShapeDtypeStruct((rows, width), f32), jax.ShapeDtypeStruct((rows, width), bf16)],
        **limits(lead),
    )(place, mixed, *weight, tokens, gain, shift)


def out_back_kernel(
    place, own_ref, x_ref, y_ref, far_ref, hidden_ref, grad_ref, gain_ref, w0_ref, w1_ref,
    mixed_ref, total_ref, low_ref, vector_ref,
):
    s = pl.program_id(0)

    @pl.when(s == 0)
    def _():
        norm_grad = own_ref[...] + x_ref[...].astype(f32) + y_ref[...].astype(f32) + far_ref[...].astype(f32)
        normed, inv_std = layer_stats(hidden_ref[...])
        vector_ref[0:1, :] = jnp.sum(norm_grad * normed, axis=0, keepdims=True)
        vector_ref[1:2, :] = jnp.sum(norm_grad, axis=0, keepdims=True)
        total = grad_ref[...].astype(f32) + norm_back(norm_grad, normed, inv_std, gain_ref[...])
        total_ref[...] = total
        low_ref[...] = total.astype(bf16)

    @pl.when(s < 4)
    def _():
        mixed_ref[0] = nt(low_ref[...], w0_ref[...]).astype(bf16)

    @pl.when(s >= 4)
    def _():
        mixed_ref[0] = nt(low_ref[...], w1_ref[...]).astype(bf16)


def out_back_rows(place, terms, hidden, out_grad, gain, weight, lead=0):
    rows, width = hidden.shape
    part = weight[0].shape[0] // 4
    whole = pl.BlockSpec((rows, width), lambda s, place: (0, 0))
    vector = pl.BlockSpec((1, width), lambda s, place: (0, 0))
    return pl.pallas_call(
        out_back_kernel,
        grid_spec=pltpu.PrefetchScalarGridSpec(
            num_scalar_prefetch=1,
            grid=(8,),
            in_specs=[*[whole] * 6, vector, *half_specs(part, width)],
            out_specs=[
                pl.BlockSpec((1, rows, part), lambda s, place: (slot_of(s, place), 0, 0)),
                whole, whole, pl.BlockSpec((2, width), lambda s, place: (0, 0)),
            ],
        ),
        out_shape=[
            jax.ShapeDtypeStruct((8, rows, part), bf16),
            jax.ShapeDtypeStruct((rows, width), f32),
            jax.ShapeDtypeStruct((rows, width), bf16),
            jax.ShapeDtypeStruct((2, width), f32),
        ],
        **limits(lead),
    )(place, *terms, hidden, out_grad, gain, *weight)


STEPS = 4


def gate_kernel(act0_ref, act1_ref, weight_ref, middle_ref, by_gate_ref, by_up_ref, act_ref):
    act = pick((act0_ref, act1_ref), STEPS)
    act_ref[...] = act
    both = nn(act, weight_ref[...])
    half = both.shape[1] // 2
    gate, up = both[:, :half], both[:, half:]
    sigmoid = jax.nn.sigmoid(gate)
    silu = gate * sigmoid
    middle_ref[...] = (silu * up).astype(bf16)
    by_gate_ref[...] = (up * (sigmoid * (1.0 + gate * (1.0 - sigmoid)))).astype(bf16)
    by_up_ref[...] = silu.astype(bf16)


def gate_rows(act, weight, lead=0):
    count, depth = act[0].shape
    count *= 2
    half, rows = weight.shape[1] // 3, count // STEPS
    out = pl.BlockSpec((rows, half), lambda s: (s, 0))
    return pl.pallas_call(
        gate_kernel,
        grid=(STEPS,),
        in_specs=[*half_specs(rows, depth, STEPS), pl.BlockSpec((depth, 2 * half), lambda s: (0, 0))],
        out_specs=[out] * 3 + [pl.BlockSpec((rows, depth), lambda s: (s, 0))],
        out_shape=[jax.ShapeDtypeStruct((count, half), bf16)] * 3 + [jax.ShapeDtypeStruct((count, depth), bf16)],
        **limits(lead),
    )(*act, weight)


def gate_back_kernel(grad0_ref, grad1_ref, weight_ref, by_gate_ref, by_up_ref, out_ref):
    middle = nn(pick((grad0_ref, grad1_ref), STEPS), weight_ref[...])
    half = middle.shape[1]
    out_ref[:, :half] = (middle * by_gate_ref[...].astype(f32)).astype(bf16)
    out_ref[:, half:] = (middle * by_up_ref[...].astype(f32)).astype(bf16)


def gate_back_rows(grad, weight, by_gate, by_up, lead=0):
    count, depth = grad[0].shape
    count *= 2
    half, rows = weight.shape[1] // 3, count // STEPS
    part = pl.BlockSpec((rows, half), lambda s: (s, 0))
    return pl.pallas_call(
        gate_back_kernel,
        grid=(STEPS,),
        in_specs=[
            *half_specs(rows, depth, STEPS), pl.BlockSpec((depth, half), lambda s: (0, 2)), part, part
        ],
        out_specs=pl.BlockSpec((rows, 2 * half), lambda s: (s, 0)),
        out_shape=jax.ShapeDtypeStruct((count, 2 * half), bf16),
        **limits(lead),
    )(*grad, weight, by_gate, by_up)


def halves(low_part, low_at, high_part, high_at):
    low_part = low_part if low_at == 0 else pltpu.roll(low_part, HEAD_DIM, 1)
    high_part = high_part if high_at else pltpu.roll(high_part, HEAD_DIM, 1)
    return jnp.where(lanes_of(low_part.shape[0]) < HEAD_DIM, low_part, high_part)


def lane_group(load, at):
    return load(at // PAIR * PAIR), at % PAIR


def split_heads_kernel(team, weight_ref, out_ref):
    def load(at):
        return weight_ref[:, at : at + PAIR].astype(f32)

    chunks = weight_ref.shape[1] // (team * HEAD_DIM)
    for p in range(team):
        for chunk in range(0, chunks, 2):
            low = lane_group(load, (chunk * team + p) * HEAD_DIM)
            high = lane_group(load, ((chunk + 1) * team + p) * HEAD_DIM)
            out_ref[p, :, chunk * HEAD_DIM : (chunk + 2) * HEAD_DIM] = halves(*low, *high).astype(bf16)


def split_heads(weight, team, lead=0):
    rows, width = weight.shape
    return pl.pallas_call(
        functools.partial(split_heads_kernel, team),
        out_shape=jax.ShapeDtypeStruct((team, rows, width // team), bf16),
        **limits(lead),
    )(weight)


def merge_heads_kernel(part_ref, out_ref):
    team = part_ref.shape[0]
    chunks = part_ref.shape[2] // HEAD_DIM
    for chunk in range(chunks):
        for p in range(0, team, 2):
            at = chunk * HEAD_DIM

            def load(at, p=p):
                return part_ref[p, :, at : at + PAIR].astype(f32)

            def load_next(at, p=p):
                return part_ref[p + 1, :, at : at + PAIR].astype(f32)

            to = (chunk * team + p) * HEAD_DIM
            out_ref[:, to : to + PAIR] = halves(*lane_group(load, at), *lane_group(load_next, at))


def merge_heads(parts, lead=0):
    team, rows, width = parts.shape
    return pl.pallas_call(
        merge_heads_kernel,
        out_shape=jax.ShapeDtypeStruct((rows, team * width), f32),
        **limits(lead),
    )(parts)


def split_ffn_kernel(team, my_ffn, *refs):
    *weight_refs, out_ref = refs
    pad = out_ref.shape[2] // len(weight_refs)
    for which, weight_ref in enumerate(weight_refs):

        def load(at):
            return weight_ref[:, at : at + PAIR].astype(f32)

        for p in range(team):
            for at in range(0, pad, PAIR):
                source = p * my_ffn + at
                low = lane_group(load, source)
                if at + HEAD_DIM < my_ffn:
                    part = halves(*low, *lane_group(load, source + HEAD_DIM))
                else:
                    part = halves(*low, jnp.zeros_like(low[0]), HEAD_DIM)
                out_ref[p, :, which * pad + at : which * pad + at + PAIR] = part.astype(bf16)


def split_ffn(weights, team, pad, lead=0):
    rows, width = weights[0].shape
    return pl.pallas_call(
        functools.partial(split_ffn_kernel, team, width // team),
        out_shape=jax.ShapeDtypeStruct((team, rows, len(weights) * pad), bf16),
        **limits(lead),
    )(*weights)


def merge_ffn_kernel(my_ffn, part_ref, *out_refs):
    team = part_ref.shape[0]
    pad = part_ref.shape[2] // len(out_refs)
    for which, out_ref in enumerate(out_refs):

        def chunk(at):
            p, inside = at // my_ffn, at % my_ffn
            return lane_group(
                lambda lane: part_ref[p, :, which * pad + lane : which * pad + lane + PAIR].astype(f32), inside
            )

        for at in range(0, team * my_ffn, PAIR):
            out_ref[:, at : at + PAIR] = halves(*chunk(at), *chunk(at + HEAD_DIM))


def merge_ffn(parts, count, ffn, lead=0):
    team, rows, width = parts.shape
    return pl.pallas_call(
        functools.partial(merge_ffn_kernel, ffn // team),
        out_shape=[jax.ShapeDtypeStruct((rows, ffn), f32)] * count,
        **limits(lead),
    )(parts)


def local(
    tokens, segments, positions, out_grad, ln1_gain, ln1_bias, qkv_weight, qkv_bias, o_weight,
    ln2_gain, ln2_bias, gate_weight, up_weight, down_weight,
):
    rows, width = tokens.shape
    shard = qkv_weight.shape[0]
    ffn = gate_weight.shape[1]
    heads = width // HEAD_DIM
    team = lax.axis_size(PLANE)
    depth = lax.axis_size("g")
    devices = team * depth
    packs = lax.axis_size("y")
    blocks = team // packs
    seq = blocks * rows
    my_heads = heads // team
    my_width = my_heads * HEAD_DIM
    my_ffn = ffn // team
    pad_ffn = -(-my_ffn // 128) * 128
    me = lax.axis_index(PLANE)
    place = jnp.stack(
        [lax.axis_index("x"), lax.axis_index("c"), lax.axis_index("y"), me]
    ).astype(jnp.int32)
    aligned = shard == HEAD_DIM

    vectors = jnp.stack([ln1_gain, ln1_bias, ln2_gain, ln2_bias], axis=0)
    vectors = jnp.concatenate([vectors, jnp.transpose(qkv_bias)], axis=0).astype(f32).reshape(-1)
    small = jnp.concatenate([vectors, segments.astype(f32), positions.astype(f32)])
    small = lax.all_to_all(
        jnp.broadcast_to(small[None], (devices, small.shape[0])), ALL, 0, 0, tiled=True
    )
    vectors = jnp.transpose(small[:, : 7 * shard].reshape(devices, 7, shard), (1, 0, 2)).reshape(7, width)
    gain_one, shift_one, gain_two, shift_two = (vectors[i][None, :] for i in range(4))
    my_plane = lax.dynamic_slice_in_dim(small[:, 7 * shard :], lax.axis_index("g") * team, team, 0)
    segment_all = my_plane[:, :rows].reshape(packs, seq)
    position_all = my_plane[:, rows:].reshape(packs, seq)
    bias_mine = lax.dynamic_slice_in_dim(
        vectors[4:7].reshape(3, my_heads, team, HEAD_DIM), me, 1, 2
    ).reshape(1, 3 * my_width)

    token_pieces = chip_pieces(tokens)
    qkv_send = after(split_heads(qkv_weight, team), small)
    qkv_mine = plane_all_to_all(qkv_send).reshape(team * shard, 3 * my_width)
    ffn_send = split_ffn([gate_weight, up_weight, down_weight], team, pad_ffn)
    ffn_send = after(ffn_send, qkv_mine, *token_pieces)
    ffn_mine = plane_all_to_all(ffn_send).reshape(team * shard, 3 * pad_ffn)

    frequency = rope_base ** (-jnp.arange(0, ROT_DIMS, 2, dtype=f32) / ROT_DIMS)
    within = jnp.arange(PAIR) % HEAD_DIM
    phases = position_all[:, :, None] * jnp.where(within < ROT_DIMS, frequency[within % (ROT_DIMS // 2)], 0.0)
    cosine = jnp.cos(phases)
    sine = jnp.sin(phases) * jnp.where(within < ROT_DIMS // 2, -1.0, 1.0)
    seg_col, seg_row = segment_all[:, :, None], segment_all[:, None, :]

    def over_g(piece):
        return lax.all_gather(piece, "g", axis=0, tiled=True)

    act_one = norm_rows(token_pieces, gain_one, shift_one)
    ffn_mine = after(ffn_mine, act_one, cosine, sine, seg_col)
    act_one = act_one, swap(act_one, "c")
    if aligned:
        out_rows = after(over_g(o_weight), ffn_mine, act_one[0])
    else:
        out_abs = lax.all_gather(o_weight, ALL, axis=0, tiled=True)
        out_abs = out_abs.reshape(my_heads, team, HEAD_DIM, width)
        out_full = [
            jnp.concatenate(
                [jnp.take(out_abs, slot_of(s, place), axis=1).reshape(my_width, width) for s in span], axis=0
            )
            for span in (range(4), range(4, 8))
        ]
    qkv_full = over_g(qkv_mine)
    ffn_full = over_g(ffn_mine)
    qkv_full = after(qkv_full, act_one[0], ffn_mine)

    qkv, act_one = project(place, act_one, qkv_full, bias_mine, cosine, sine, lead=40)
    mixed, mixed_halves, totals = attention(place, qkv, blocks, seg_col, seg_row, lead=40)
    if aligned:
        out_full = halves_of(chip_pieces(out_rows, qkv), mixed)
    hidden, act_two = out_rows_of(
        place, plane_all_to_all(mixed.reshape(team, rows, my_width)), out_full, tokens, gain_two, shift_two
    )

    act_two = halves_of(chip_pieces(act_two))
    cotangent = halves_of(chip_pieces(after(out_grad, act_two[0])))
    middle_low, by_gate, by_up, act_all = gate_rows(act_two, ffn_full)
    down_sum = row_sum(cotangent, (middle_low[: 4 * rows], middle_low[4 * rows :]))

    def own_rows(grad_sum):
        return lax.psum_scatter(grad_sum, "g", scatter_dimension=0, tiled=True)

    def back_to_rows(columns):
        return plane_all_to_all(columns.reshape(team, shard, columns.shape[1]))

    gate_up_grad = gate_back_rows(after(cotangent, down_sum), ffn_full, by_gate, by_up)
    norm_two_other = plane_send(gate_up_grad, ffn_full, 0)
    norm_two_kept = plane_keep(gate_up_grad, ffn_full, 0, norm_two_other, bf16)
    gate_up_sum = row_sum([act_all], [after(gate_up_grad, norm_two_kept[0])], lead=60)
    down_own = own_rows(down_sum)
    gate_up_own = own_rows(gate_up_sum)
    norm_two_terms = plane_direct(norm_two_kept)
    output_other = plane_send(after(middle_low, gate_up_sum), ffn_full, 2)
    output_kept = plane_keep(middle_low, ffn_full, 2, output_other)
    norm_two_terms = after(norm_two_terms, output_kept[0], down_own)
    mixed_grad, hidden_grad, hidden_low, two_sums = out_back_rows(
        place, norm_two_terms, hidden, out_grad, gain_two, out_full
    )

    output_terms = plane_corner(after(output_kept, mixed_grad))
    mixed_grad = plane_all_to_all(mixed_grad).reshape(packs, blocks, rows, my_width)
    mixed_grad = after(mixed_grad, output_terms)
    qkv_grad = attention_back(place, qkv, mixed_grad, totals, cosine, sine, seg_col, seg_row, lead=40)
    qkv_grad = qkv_grad.reshape(8 * rows, 3 * my_width)
    output = (hidden + total_of(plane_neighbours(output_terms))).astype(bf16)
    qkv_sum = row_sum([act_one], [after(qkv_grad, output)], lead=40)
    qkv_own = own_rows(qkv_sum)
    norm_one_other = plane_send(after(qkv_grad, qkv_sum, gate_up_own), qkv_full, 0)
    hidden_pieces = chip_pieces(after(hidden_low, qkv_grad), norm_one_other)
    norm_one_kept = plane_keep(qkv_grad, qkv_full, 0, norm_one_other, bf16, lead=30)
    hidden_all = halves_of(hidden_pieces, norm_one_kept[0], lead=60)
    mixed_halves = mixed_halves.reshape(2, 4 * rows, my_width)
    out_sum = row_sum((mixed_halves[0], mixed_halves[1]), hidden_all)
    if aligned and depth == 4:
        out_share = deep_reduce(out_sum.reshape(4, shard, width))
    elif aligned:
        out_share = own_rows(out_sum).astype(f32)
    else:
        spread = jnp.zeros((my_heads, team, HEAD_DIM, width), bf16)
        spread = lax.dynamic_update_slice_in_dim(
            spread, out_sum.reshape(my_heads, 1, HEAD_DIM, width), me, 1
        )
        out_share = lax.psum_scatter(
            spread.reshape(width, width).astype(f32), ALL, scatter_dimension=0, tiled=True
        )
    down_share = merge_ffn(back_to_rows(after(down_own, qkv_sum)), 1, ffn)
    gate_up_share = merge_ffn(back_to_rows(gate_up_own), 2, ffn)
    norm_grad_one = total_of(
        after(plane_direct(norm_one_kept), qkv_own, out_share, down_share, gate_up_share)
    )
    normed_one, inv_one = layer_stats(tokens.astype(f32))
    input_grad = (hidden_grad + norm_back(norm_grad_one, normed_one, inv_one, gain_one)).astype(bf16)

    bias_sum = jnp.sum(qkv_grad.astype(f32), axis=0).reshape(3, my_heads, 1, HEAD_DIM)
    mine = (jnp.arange(team) == me).astype(f32)[None, None, :, None]
    terms = jnp.concatenate(
        [
            jnp.sum(norm_grad_one * normed_one, axis=0)[None],
            jnp.sum(norm_grad_one, axis=0)[None],
            (bias_sum * mine).reshape(3, width),
            two_sums,
        ],
        axis=0,
    )
    terms = jnp.transpose(terms.reshape(7, devices, shard), (1, 0, 2)).reshape(devices, 7 * shard)
    vector_share = jnp.sum(lax.all_to_all(terms, ALL, 0, 0, tiled=True), axis=0).reshape(7, shard)
    qkv_share = merge_heads(back_to_rows(qkv_own))
    return (
        output,
        input_grad,
        vector_share[0],
        vector_share[1],
        qkv_share,
        jnp.transpose(vector_share[2:5]),
        out_share,
        vector_share[5],
        vector_share[6],
        *gate_up_share,
        *down_share,
    )


def solution(mesh):
    dp, ctx = mesh.shape["dp"], mesh.shape["ctx"]
    split = Mesh(mesh.devices.reshape(dp // 2, 2, ctx // 2, 2), ALL)
    row, flat = P(ALL, None), P(ALL)
    return jax.shard_map(
        local,
        mesh=split,
        in_specs=(row, flat, flat, row, flat, flat, row, row, row, flat, flat, row, row, row),
        out_specs=(row, row, flat, flat, row, row, row, flat, flat, row, row, row),
        check_vma=False,
    )
```

```python
import functools

import jax
import jax.numpy as jnp
from jax import lax
from jax.experimental import pallas as pl
from jax.experimental.pallas import tpu as pltpu
from jax.sharding import Mesh
from jax.sharding import PartitionSpec as P

HEAD_DIM = 64
ROT_DIMS = 16
PAIR = 2 * HEAD_DIM
PLANE = ("y", "x", "c")
ALL = ("g", "y", "x", "c")
bf16 = jnp.bfloat16
f32 = jnp.float32

epsilon = 1e-05
neg_large = -1e30
rope_base = 10000.0
score_scale = 0.125


def layer_stats(values):
    mean_value = jnp.mean(values, axis=-1, keepdims=True)
    centered = values - mean_value
    inv_std = lax.rsqrt(jnp.mean(centered * centered, axis=-1, keepdims=True) + epsilon)
    return (centered * inv_std, inv_std)


def norm_back(grad_rows, normed, inv_std, gain_row):
    scaled = grad_rows * gain_row
    inner = jnp.mean(scaled * normed, axis=-1, keepdims=True)
    return inv_std * (scaled - jnp.mean(scaled, axis=-1, keepdims=True) - normed * inner)


def contract(left, right, left_dim, right_dim, kind=f32):
    return lax.dot_general(
        left, right, (((left_dim,), (right_dim,)), ((), ())), preferred_element_type=f32
    ).astype(kind)


def after(values, *others):
    return lax.optimization_barrier((values, *others))[0]


def fenced(function, *operands):
    shapes = jax.eval_shape(function, *operands)
    return lax.cond(
        lax.axis_index("g") < lax.axis_size("g"),
        function,
        lambda *_: jax.tree.map(lambda leaf: jnp.zeros(leaf.shape, leaf.dtype), shapes),
        *operands,
    )


def swap(values, axis):
    return lax.ppermute(values, axis, [(0, 1), (1, 0)])


def join_kernel(*refs):
    *piece_refs, out_ref = refs
    at = 0
    for piece in piece_refs:
        out_ref[at : at + piece.shape[0], :] = piece[...]
        at += piece.shape[0]


def join(pieces, time=5):
    rows, width = sum(piece.shape[0] for piece in pieces), pieces[0].shape[1]
    return pl.pallas_call(
        join_kernel,
        grid=(4,),
        in_specs=[pl.BlockSpec((piece.shape[0], width // 4), lambda i: (0, i)) for piece in pieces],
        out_specs=pl.BlockSpec((rows, width // 4), lambda i: (0, i)),
        out_shape=jax.ShapeDtypeStruct((rows, width), pieces[0].dtype),
        **limits(time),
    )(*pieces)


def near_pieces(rows):
    return swap(rows, "x"), swap(rows, "y")


def chip_pieces(rows, *first, near=None):
    half = rows.shape[0] // 2
    over_x, over_y = near or near_pieces(rows)
    if first:
        over_x, over_y = lax.optimization_barrier((over_x, over_y, *first))[:2]
    return [rows, over_x, over_y, swap(over_y[:half], "x"), swap(over_x[half:], "y")]


def halves_of(pieces, *first, time=5):
    if first:
        pieces = lax.optimization_barrier((*pieces, *first))[: len(pieces)]
    mine = join(pieces, time)
    return mine, swap(mine, "c")


def send_kernel(left_ref, right_ref, out_ref):
    out_ref[...] = nt(left_ref[...], right_ref[...]).astype(bf16)


def keep_kernel(left_ref, right_ref, other_ref, corner_ref, x_ref, y_ref, own_ref):
    s = pl.program_id(0)
    total = nt(left_ref[...], right_ref[...]) + other_ref[...].astype(f32)

    @pl.when(s == 0)
    def _():
        corner_ref[...] = total.astype(bf16)

    for which, ref in ((1, x_ref), (2, y_ref), (3, own_ref)):

        @pl.when(s == which)
        def _(ref=ref):
            ref[...] = total.astype(ref.dtype)


def corner_first(s):
    return jnp.where(s == 0, 3, jnp.where(s == 3, 0, s))


def columns_of(right, at, depth):
    if right.shape[1] == depth:
        return pl.BlockSpec(right.shape, lambda s: (0, 0))
    return pl.BlockSpec((pl.Element(right.shape[0]), pl.Element(depth)), lambda s: (0, at))


def plane_send(left, right, at, time=None):
    rows, depth, width = left.shape[0] // 8, left.shape[1], right.shape[0]
    terms = pl.pallas_call(
        send_kernel,
        grid=(2,),
        in_specs=[
            pl.BlockSpec((2 * rows, depth), lambda s: (s + 2, 0)),
            columns_of(right, at, depth),
        ],
        out_specs=pl.BlockSpec((2 * rows, width), lambda s: (s, 0)),
        out_shape=jax.ShapeDtypeStruct((4 * rows, width), bf16),
        **limits(depth // 134 if time is None else time),
    )(left, right)
    return swap(terms, "c")


def plane_keep(left, right, at, other, kind=f32, time=None):
    rows, depth, width = left.shape[0] // 8, left.shape[1], right.shape[0]
    whole = pl.BlockSpec((rows, width), lambda s: (0, 0))
    return pl.pallas_call(
        keep_kernel,
        grid=(4,),
        in_specs=[
            pl.BlockSpec((rows, depth), lambda s: (corner_first(s), 0)),
            columns_of(right, at, depth),
            pl.BlockSpec((rows, width), lambda s: (corner_first(s), 0)),
        ],
        out_specs=[whole] * 4,
        out_shape=[jax.ShapeDtypeStruct((rows, width), kind) for kind in (bf16, kind, kind, f32)],
        **limits(depth // 114 if time is None else time),
    )(left, right, other)


def plane_direct(kept):
    corner, for_x, for_y, own = kept
    far = lax.ppermute(corner, ("y", "x"), [(0, 3), (1, 2), (2, 1), (3, 0)])
    return own, swap(for_x, "x"), swap(for_y, "y"), far


def plane_corner(kept):
    corner, for_x, for_y, own = kept
    half = corner.shape[0] // 2
    from_x = swap(corner[:half], "x")
    from_y = swap(corner[half:], "y")
    to_x = jnp.concatenate([for_x[:half], for_x[half:] + from_y.astype(f32)], axis=0).astype(bf16)
    to_y = jnp.concatenate([for_y[:half] + from_x.astype(f32), for_y[half:]], axis=0).astype(bf16)
    return own, to_x, to_y


def plane_neighbours(terms):
    own, to_x, to_y = terms
    return own, swap(to_x, "x"), swap(to_y, "y")


def total_of(terms):
    return sum(term.astype(f32) for term in terms[1:]) + terms[0]


def sum_kernel(*refs):
    *left_refs, right_ref, out_ref = refs
    total, at = None, 0
    for left_ref in left_refs:
        part = tn(left_ref[...], right_ref[at : at + left_ref.shape[0], :])
        total = part if total is None else total + part
        at += left_ref.shape[0]
    out_ref[...] = total[:, : out_ref.shape[1]].astype(bf16)


def row_sum(left, right, kept=None, time=None):
    width, (rows, columns) = left[0].shape[1], right.shape
    kept = kept or columns
    step = min(width, 512)
    return pl.pallas_call(
        sum_kernel,
        grid=(width // step,),
        in_specs=[
            *[pl.BlockSpec((piece.shape[0], step), lambda i: (0, i)) for piece in left],
            pl.BlockSpec((rows, columns), lambda i: (0, 0)),
        ],
        out_specs=pl.BlockSpec((step, kept), lambda i: (i, 0)),
        out_shape=jax.ShapeDtypeStruct((width, kept), bf16),
        **limits(columns // 83 if time is None else time),
    )(*left, right)


def pair_kernel(left0_ref, left1_ref, right0_ref, right1_ref, out_ref):
    out_ref[...] = (tn(left0_ref[0], right0_ref[...]) + tn(left1_ref[0], right1_ref[...])).astype(bf16)


def pair_sum(left, right, time):
    _, rows, width = left.shape
    columns = right[0].shape[1]
    step = columns // 4
    return pl.pallas_call(
        pair_kernel,
        grid=(4,),
        in_specs=[
            pl.BlockSpec((1, rows, width), lambda i: (0, 0, 0)),
            pl.BlockSpec((1, rows, width), lambda i: (1, 0, 0)),
            pl.BlockSpec((rows, step), lambda i: (0, i)),
            pl.BlockSpec((rows, step), lambda i: (0, i)),
        ],
        out_specs=pl.BlockSpec((width, step), lambda i: (0, i)),
        out_shape=jax.ShapeDtypeStruct((width, columns), bf16),
        **limits(time),
    )(left, left, *right)


def plane_all_to_all(blocks):
    return lax.all_to_all(blocks, PLANE, 0, 0, tiled=True)


def turned(rows, cosine, sine, first):
    partner = jnp.where(first, pltpu.roll(rows, PAIR - ROT_DIMS // 2, 1), pltpu.roll(rows, ROT_DIMS // 2, 1))
    return rows * cosine + partner * sine


def lanes_of(rows):
    return lax.broadcasted_iota(jnp.int32, (rows, PAIR), 1)


def keep_head(values, head):
    lane = lanes_of(values.shape[0])
    inside = lane < HEAD_DIM if head == 0 else lane >= HEAD_DIM
    return jnp.where(inside, values, jnp.zeros_like(values))


def allowed_block(seg_col, seg_row, block, rows):
    same = seg_col[0, : (block + 1) * rows, :] == seg_row[0, :, block * rows : (block + 1) * rows]
    key_at = lax.broadcasted_iota(jnp.int32, same.shape, 0)
    query_at = lax.broadcasted_iota(jnp.int32, same.shape, 1) + block * rows
    return same & (key_at <= query_at)


def where_is(place, block):
    return jnp.bitwise_xor(place[1], block % 2), jnp.bitwise_xor(place[0], block // 2)


def nt(left, right):
    return lax.dot_general(left, right, (((1,), (1,)), ((), ())), preferred_element_type=f32)


def tn(left, right):
    return lax.dot_general(left, right, (((0,), (0,)), ((), ())), preferred_element_type=f32)


def nn(left, right):
    return lax.dot_general(left, right, (((1,), (0,)), ((), ())), preferred_element_type=f32)


def attend_kernel(
    blocks, place, query_ref, key_ref, value_ref, col_ref, row_ref, mixed_ref, halves_ref, total_ref,
):
    rows = mixed_ref.shape[2]
    for block in range(blocks):
        span = slice(block * rows, (block + 1) * rows)
        upto = (block + 1) * rows
        allowed = allowed_block(col_ref, row_ref, block, rows)
        mixed = jnp.zeros((PAIR, rows), f32)
        for head in range(2):
            query = keep_head(query_ref[0, span, :], head) * score_scale
            scores = jnp.where(allowed, nt(key_ref[0, :upto, :], query), neg_large)
            top = jnp.max(scores, axis=0, keepdims=True)
            weights = jnp.exp(scores - top)
            total = jnp.sum(weights, axis=0, keepdims=True)
            probs = (weights * (1.0 / total)).astype(bf16)
            mixed = mixed + tn(keep_head(value_ref[0, :upto, :], head), probs)
            total_ref[0, 0, head : head + 1, span] = top + jnp.log(total)
        mixed = jnp.transpose(mixed).astype(bf16)
        mixed_ref[0, block] = mixed
        half, entry = where_is(place, block)
        halves_ref[half, 0, entry] = mixed


def attend_back_kernel(
    blocks, place, query_ref, key_ref, value_ref, grad_ref, total_ref, cos_ref, sin_ref, col_ref, row_ref,
    out_ref, dk_ref, dv_ref,
):
    pair = pl.program_id(1)
    rows = grad_ref.shape[2]
    width = out_ref.shape[4] // 3
    first = lanes_of(rows) % HEAD_DIM < ROT_DIMS // 2

    def put(block, which, values):
        half, entry = where_is(place, block)
        at = pl.multiple_of(which * width + pair * PAIR, PAIR)
        out_ref[half, 0, entry, :, pl.ds(at, PAIR)] = values.astype(bf16)

    dk_ref[...] = jnp.zeros_like(dk_ref)
    dv_ref[...] = jnp.zeros_like(dv_ref)
    for block in range(blocks):
        span = slice(block * rows, (block + 1) * rows)
        upto = (block + 1) * rows
        allowed = allowed_block(col_ref, row_ref, block, rows)
        dq = jnp.zeros((PAIR, rows), f32)
        for head in range(2):
            query = keep_head(query_ref[0, span, :], head) * score_scale
            grad = keep_head(grad_ref[0, block], head)
            scores = jnp.where(allowed, nt(key_ref[0, :upto, :], query), neg_large)
            probs = jnp.exp(scores - total_ref[0, 0, head : head + 1, span])
            prob_grad = nt(value_ref[0, :upto, :], grad)
            inner = jnp.sum(probs * prob_grad, axis=0, keepdims=True)
            score_grad = (probs * (prob_grad - inner)).astype(bf16)
            dk_ref[:upto, :] += nn(score_grad, query)
            dv_ref[:upto, :] += nn(probs.astype(bf16), grad)
            dq = dq + tn(keep_head(key_ref[0, :upto, :], head), score_grad)
        put(block, 0, turned(jnp.transpose(dq) * score_scale, cos_ref[0, span, :], -sin_ref[0, span, :], first))
    for block in range(blocks):
        span = slice(block * rows, (block + 1) * rows)
        put(block, 1, turned(dk_ref[span, :], cos_ref[0, span, :], -sin_ref[0, span, :], first))
        put(block, 2, dv_ref[span, :])


SHORT = 6


def limits(time):
    return dict(
        compiler_params=pltpu.CompilerParams(vmem_limit_bytes=56 * 1024 * 1024),
        cost_estimate=pl.CostEstimate(flops=time * 10**9 // SHORT, bytes_accessed=time * 3 * 10**6 // SHORT, transcendentals=0),
    )


def qkv_parts(seq, pairs):
    return [
        pl.BlockSpec((1, seq, PAIR), lambda p, h, place, which=which: (p, 0, which * pairs + h))
        for which in range(3)
    ]


def at_pack(*shape):
    rest = (0,) * len(shape)
    return pl.BlockSpec((1, *shape), lambda p, h, place: (jnp.bitwise_xor(p, place[2]), *rest))


def attention(place, qkv, blocks, seg_col, seg_row):
    packs, seq, width = qkv.shape
    width //= 3
    rows, pairs = seq // blocks, width // PAIR
    return pl.pallas_call(
        functools.partial(attend_kernel, blocks),
        grid_spec=pltpu.PrefetchScalarGridSpec(
            num_scalar_prefetch=1,
            grid=(packs, pairs),
            in_specs=[*qkv_parts(seq, pairs), at_pack(seq, 1), at_pack(1, seq)],
            out_specs=[
                pl.BlockSpec(
                    (1, blocks, rows, PAIR), lambda p, h, place: (jnp.bitwise_xor(p, place[2]), 0, 0, h)
                ),
                pl.BlockSpec((2, 1, 2, rows, PAIR), lambda p, h, place: (0, p, 0, 0, h)),
                pl.BlockSpec((1, 1, 2, seq), lambda p, h, place: (p, h, 0, 0)),
            ],
        ),
        out_shape=[
            jax.ShapeDtypeStruct((packs, blocks, rows, width), bf16),
            jax.ShapeDtypeStruct((2, packs, 2, rows, width), bf16),
            jax.ShapeDtypeStruct((packs, pairs, 2, seq), f32),
        ],
        **limits(16),
    )(place, qkv, qkv, qkv, seg_col, seg_row)


def attention_back(place, qkv, grad, totals, cosine, sine, seg_col, seg_row, time=25):
    packs, blocks, rows, width = grad.shape
    pairs, seq = width // PAIR, blocks * rows
    return pl.pallas_call(
        functools.partial(attend_back_kernel, blocks),
        grid_spec=pltpu.PrefetchScalarGridSpec(
            num_scalar_prefetch=1,
            grid=(packs, pairs),
            in_specs=[
                *qkv_parts(seq, pairs),
                pl.BlockSpec(
                    (1, blocks, rows, PAIR), lambda p, h, place: (jnp.bitwise_xor(p, place[2]), 0, 0, h)
                ),
                pl.BlockSpec((1, 1, 2, seq), lambda p, h, place: (p, h, 0, 0)),
                at_pack(seq, PAIR), at_pack(seq, PAIR), at_pack(seq, 1), at_pack(1, seq),
            ],
            out_specs=pl.BlockSpec((2, 1, 2, rows, 3 * width), lambda p, h, place: (0, p, 0, 0, 0)),
            scratch_shapes=[pltpu.VMEM((seq, PAIR), f32)] * 2,
        ),
        out_shape=jax.ShapeDtypeStruct((2, packs, 2, rows, 3 * width), bf16),
        **limits(time),
    )(place, qkv, qkv, qkv, grad, totals, cosine, sine, seg_col, seg_row)


def norm_kernel(*refs):
    *piece_refs, gain_ref, shift_ref, act_ref = refs
    step, at = 64, 0
    for piece in piece_refs:
        for row in range(0, piece.shape[0], step):
            normed = layer_stats(piece[row : row + step, :].astype(f32))[0]
            act_ref[at : at + step, :] = (normed * gain_ref[...] + shift_ref[...]).astype(bf16)
            at += step


def norm_rows(pieces, gain, shift):
    count, width = sum(piece.shape[0] for piece in pieces), gain.shape[1]
    return pl.pallas_call(
        norm_kernel,
        out_shape=jax.ShapeDtypeStruct((count, width), bf16),
        **limits(7),
    )(*pieces, gain, shift)


def pick(halves, steps):
    return jnp.where(pl.program_id(0) < steps // 2, halves[0][...], halves[1][...])


def project_kernel(place, act0_ref, act1_ref, weight_ref, bias_ref, cos_ref, sin_ref, out_ref, act_ref):
    act = pick((act0_ref, act1_ref), 8)
    act_ref[...] = act
    projected = nn(act, weight_ref[...]) + bias_ref[...]
    rows, width = projected.shape
    first = lanes_of(rows) % HEAD_DIM < ROT_DIMS // 2
    cosine, sine = cos_ref[0], sin_ref[0]
    for at in range(0, width, PAIR):
        part = projected[:, at : at + PAIR]
        if at < 2 * width // 3:
            part = turned(part, cosine, sine, first)
        out_ref[0, :, at : at + PAIR] = part.astype(bf16)


def project(place, act, weight, bias, cosine, sine):
    count, depth = act[0].shape
    width = weight.shape[1]
    packs, seq, _ = cosine.shape
    rows = count // 4

    def block_of(s, place):
        return jnp.bitwise_xor(place[0], s % 2) * 2 + jnp.bitwise_xor(place[1], s // 4)

    def table(s, place):
        return (jnp.bitwise_xor(place[2], s // 2 % 2), block_of(s, place), 0)

    return pl.pallas_call(
        project_kernel,
        grid_spec=pltpu.PrefetchScalarGridSpec(
            num_scalar_prefetch=1,
            grid=(8,),
            in_specs=[
                *half_specs(rows, depth),
                pl.BlockSpec((depth, width), lambda s, place: (0, 0)),
                pl.BlockSpec((1, width), lambda s, place: (0, 0)),
                pl.BlockSpec((1, rows, PAIR), table),
                pl.BlockSpec((1, rows, PAIR), table),
            ],
            out_specs=[
                pl.BlockSpec((1, rows, width), lambda s, place: (s // 2 % 2, block_of(s, place), 0)),
                pl.BlockSpec((rows, depth), lambda s, place: (s, 0)),
            ],
        ),
        out_shape=[
            jax.ShapeDtypeStruct((packs, seq, width), bf16), jax.ShapeDtypeStruct((2 * count, depth), bf16)
        ],
        **limits(15),
    )(place, *act, weight, bias, cosine, sine)


def slot_of(s, place):
    return jnp.bitwise_xor(place[3], s // 4 + (s // 2 % 2) * 4 + (s % 2) * 2)


def half_specs(rows, width, steps=8):
    half = steps // 2
    return [
        pl.BlockSpec((rows, width), lambda s, *place: (jnp.minimum(s, half - 1), 0)),
        pl.BlockSpec((rows, width), lambda s, *place: (jnp.maximum(s - half, 0), 0)),
    ]


def out_kernel(place, mixed_ref, w0_ref, w1_ref, token_ref, gain_ref, shift_ref, hidden_ref, act_ref, sum_ref):
    s = pl.program_id(0)

    @pl.when(s == 0)
    def _():
        sum_ref[...] = token_ref[...].astype(f32)

    @pl.when(s < 4)
    def _():
        sum_ref[...] += nn(mixed_ref[0], w0_ref[...])

    @pl.when(s >= 4)
    def _():
        sum_ref[...] += nn(mixed_ref[0], w1_ref[...])

    @pl.when(s == 7)
    def _():
        hidden = sum_ref[...]
        hidden_ref[...] = hidden
        act_ref[...] = (layer_stats(hidden)[0] * gain_ref[...] + shift_ref[...]).astype(bf16)


def out_rows_of(place, mixed, weight, tokens, gain, shift):
    rows, width = tokens.shape
    part = mixed.shape[2]
    whole = pl.BlockSpec((rows, width), lambda s, place: (0, 0))
    vector = pl.BlockSpec((1, width), lambda s, place: (0, 0))
    return pl.pallas_call(
        out_kernel,
        grid_spec=pltpu.PrefetchScalarGridSpec(
            num_scalar_prefetch=1,
            grid=(8,),
            in_specs=[
                pl.BlockSpec((1, rows, part), lambda s, place: (slot_of(s, place), 0, 0)),
                *half_specs(part, width), whole, vector, vector,
            ],
            out_specs=[whole, whole],
            scratch_shapes=[pltpu.VMEM((rows, width), f32)],
        ),
        out_shape=[jax.ShapeDtypeStruct((rows, width), f32), jax.ShapeDtypeStruct((rows, width), bf16)],
        **limits(12),
    )(place, mixed, *weight, tokens, gain, shift)


def out_back_kernel(
    place, own_ref, x_ref, y_ref, far_ref, hidden_ref, grad_ref, gain_ref, w0_ref, w1_ref,
    mixed_ref, total_ref, low_ref, vector_ref,
):
    s = pl.program_id(0)

    @pl.when(s == 0)
    def _():
        norm_grad = own_ref[...] + x_ref[...].astype(f32) + y_ref[...].astype(f32) + far_ref[...].astype(f32)
        normed, inv_std = layer_stats(hidden_ref[...])
        vector_ref[0:1, :] = jnp.sum(norm_grad * normed, axis=0, keepdims=True)
        vector_ref[1:2, :] = jnp.sum(norm_grad, axis=0, keepdims=True)
        total = grad_ref[...].astype(f32) + norm_back(norm_grad, normed, inv_std, gain_ref[...])
        total_ref[...] = total
        low_ref[...] = total.astype(bf16)

    @pl.when(s < 4)
    def _():
        mixed_ref[0] = nt(low_ref[...], w0_ref[...]).astype(bf16)

    @pl.when(s >= 4)
    def _():
        mixed_ref[0] = nt(low_ref[...], w1_ref[...]).astype(bf16)


def out_back_rows(place, terms, hidden, out_grad, gain, weight, time=15):
    rows, width = hidden.shape
    part = weight[0].shape[0] // 4
    whole = pl.BlockSpec((rows, width), lambda s, place: (0, 0))
    vector = pl.BlockSpec((1, width), lambda s, place: (0, 0))
    return pl.pallas_call(
        out_back_kernel,
        grid_spec=pltpu.PrefetchScalarGridSpec(
            num_scalar_prefetch=1,
            grid=(8,),
            in_specs=[*[whole] * 6, vector, *half_specs(part, width)],
            out_specs=[
                pl.BlockSpec((1, rows, part), lambda s, place: (slot_of(s, place), 0, 0)),
                whole, whole, pl.BlockSpec((2, width), lambda s, place: (0, 0)),
            ],
        ),
        out_shape=[
            jax.ShapeDtypeStruct((8, rows, part), bf16),
            jax.ShapeDtypeStruct((rows, width), f32),
            jax.ShapeDtypeStruct((rows, width), bf16),
            jax.ShapeDtypeStruct((2, width), f32),
        ],
        **limits(time),
    )(place, *terms, hidden, out_grad, gain, *weight)


STEPS = 4


def gate_kernel(act0_ref, act1_ref, weight_ref, middle_ref, by_gate_ref, by_up_ref, act_ref):
    act = pick((act0_ref, act1_ref), STEPS)
    act_ref[...] = act
    both = nn(act, weight_ref[...])
    half, wide = both.shape[1] // 2, middle_ref.shape[1]
    inside = lax.broadcasted_iota(jnp.int32, (both.shape[0], wide), 1) < half
    gate = jnp.where(inside, both[:, :wide], 0.0)
    up = jnp.where(inside, pltpu.roll(both[:, 2 * half - wide :], half, 1), 0.0)
    sigmoid = jax.nn.sigmoid(gate)
    silu = gate * sigmoid
    middle_ref[...] = (silu * up).astype(bf16)
    by_gate_ref[...] = (up * (sigmoid * (1.0 + gate * (1.0 - sigmoid)))).astype(bf16)
    by_up_ref[...] = silu.astype(bf16)


def gate_rows(act, weight, half):
    count, depth = act[0].shape
    count *= 2
    wide, rows = -(-half // PAIR) * PAIR, count // STEPS
    out = pl.BlockSpec((rows, wide), lambda s: (s, 0))
    return pl.pallas_call(
        gate_kernel,
        grid=(STEPS,),
        in_specs=[*half_specs(rows, depth, STEPS), pl.BlockSpec((depth, 2 * half), lambda s: (0, 0))],
        out_specs=[out] * 3 + [pl.BlockSpec((rows, depth), lambda s: (s, 0))],
        out_shape=[jax.ShapeDtypeStruct((count, wide), bf16)] * 3 + [jax.ShapeDtypeStruct((count, depth), bf16)],
        **limits(20),
    )(*act, weight)


def gate_back_kernel(grad0_ref, grad1_ref, weight_ref, by_gate_ref, by_up_ref, out_ref):
    middle = nn(pick((grad0_ref, grad1_ref), STEPS), weight_ref[...])
    gate = middle * by_gate_ref[...].astype(f32)
    half, wide = out_ref.shape[1] // 2, middle.shape[1]
    up = pltpu.roll(middle * by_up_ref[...].astype(f32), half - (2 * half - wide), 1)
    cut = 2 * half - wide
    out_ref[:, :cut] = gate[:, :cut].astype(bf16)
    out_ref[:, cut:wide] = (gate[:, cut:] + up[:, : wide - cut]).astype(bf16)
    out_ref[:, wide:] = up[:, wide - cut :].astype(bf16)


def gate_back_rows(grad, weight, by_gate, by_up, half):
    count, depth = grad[0].shape
    count *= 2
    wide, rows = by_gate.shape[1], count // STEPS
    part = pl.BlockSpec((rows, wide), lambda s: (s, 0))
    return pl.pallas_call(
        gate_back_kernel,
        grid=(STEPS,),
        in_specs=[
            *half_specs(rows, depth, STEPS), columns_of(weight, 2 * half, wide), part, part
        ],
        out_specs=pl.BlockSpec((rows, 2 * half), lambda s: (s, 0)),
        out_shape=jax.ShapeDtypeStruct((count, 2 * half), bf16),
        **limits(13),
    )(*grad, weight, by_gate, by_up)


def halves(low_part, low_at, high_part, high_at):
    low_part = low_part if low_at == 0 else pltpu.roll(low_part, HEAD_DIM, 1)
    high_part = high_part if high_at else pltpu.roll(high_part, HEAD_DIM, 1)
    return jnp.where(lanes_of(low_part.shape[0]) < HEAD_DIM, low_part, high_part)


def lane_group(load, at):
    return load(at // PAIR * PAIR), at % PAIR


def split_heads_kernel(team, weight_ref, out_ref):
    def load(at):
        return weight_ref[:, at : at + PAIR].astype(f32)

    chunks = weight_ref.shape[1] // (team * HEAD_DIM)
    for p in range(team):
        for chunk in range(0, chunks, 2):
            low = lane_group(load, (chunk * team + p) * HEAD_DIM)
            high = lane_group(load, ((chunk + 1) * team + p) * HEAD_DIM)
            out_ref[p, :, chunk * HEAD_DIM : (chunk + 2) * HEAD_DIM] = halves(*low, *high).astype(bf16)


def split_heads(weight, team):
    rows, width = weight.shape
    return pl.pallas_call(
        functools.partial(split_heads_kernel, team),
        out_shape=jax.ShapeDtypeStruct((team, rows, width // team), bf16),
        **limits(2),
    )(weight)


def merge_heads_kernel(part_ref, out_ref):
    team = part_ref.shape[0]
    chunks = part_ref.shape[2] // HEAD_DIM
    for chunk in range(chunks):
        for p in range(0, team, 2):
            at = chunk * HEAD_DIM

            def load(at, p=p):
                return part_ref[p, :, at : at + PAIR].astype(f32)

            def load_next(at, p=p):
                return part_ref[p + 1, :, at : at + PAIR].astype(f32)

            to = (chunk * team + p) * HEAD_DIM
            out_ref[:, to : to + PAIR] = halves(*lane_group(load, at), *lane_group(load_next, at))


def merge_heads(parts):
    team, rows, width = parts.shape
    return pl.pallas_call(
        merge_heads_kernel,
        out_shape=jax.ShapeDtypeStruct((rows, team * width), f32),
        **limits(2),
    )(parts)


def split_ffn_kernel(team, my_ffn, *refs):
    *weight_refs, out_ref = refs
    steps = my_ffn // HEAD_DIM

    def chunk(p, at):
        which, inside = at // steps, at % steps * HEAD_DIM
        if which == len(weight_refs):
            return jnp.zeros((out_ref.shape[1], PAIR), f32), at % 2 * HEAD_DIM
        return lane_group(
            lambda lane: weight_refs[which][:, lane : lane + PAIR].astype(f32), p * my_ffn + inside
        )

    for p in range(team):
        for at in range(0, out_ref.shape[2], PAIR):
            first = at // HEAD_DIM
            out_ref[p, :, at : at + PAIR] = halves(*chunk(p, first), *chunk(p, first + 1)).astype(bf16)


def split_ffn(weights, team, packed):
    rows, width = weights[0].shape
    return pl.pallas_call(
        functools.partial(split_ffn_kernel, team, width // team),
        out_shape=jax.ShapeDtypeStruct((team, rows, packed), bf16),
        **limits(3),
    )(*weights)


def merge_ffn_kernel(my_ffn, part_ref, *out_refs):
    team = part_ref.shape[0]
    for which, out_ref in enumerate(out_refs):

        def chunk(at):
            p, inside = at // my_ffn, at % my_ffn
            group, lane = (which * my_ffn + inside) // PAIR * PAIR, (which * my_ffn + inside) % PAIR
            return part_ref[p, :, group : group + PAIR].astype(f32), lane

        for at in range(0, team * my_ffn, PAIR):
            out_ref[:, at : at + PAIR] = halves(*chunk(at), *chunk(at + HEAD_DIM))


def merge_ffn(parts, count, ffn):
    team, rows, width = parts.shape
    parts = jnp.pad(parts, ((0, 0), (0, 0), (0, -width % PAIR)))
    return pl.pallas_call(
        functools.partial(merge_ffn_kernel, ffn // team),
        out_shape=[jax.ShapeDtypeStruct((rows, ffn), f32)] * count,
        **limits(3),
    )(parts)


def local(
    tokens, segments, positions, out_grad, ln1_gain, ln1_bias, qkv_weight, qkv_bias, o_weight,
    ln2_gain, ln2_bias, gate_weight, up_weight, down_weight,
):
    rows, width = tokens.shape
    shard = qkv_weight.shape[0]
    ffn = gate_weight.shape[1]
    heads = width // HEAD_DIM
    team = lax.axis_size(PLANE)
    depth = lax.axis_size("g")
    devices = team * depth
    packs = lax.axis_size("y")
    blocks = team // packs
    seq = blocks * rows
    my_heads = heads // team
    my_width = my_heads * HEAD_DIM
    my_ffn = ffn // team
    packed = -(-3 * my_ffn // PAIR) * PAIR
    me = lax.axis_index(PLANE)
    place = jnp.stack(
        [lax.axis_index("x"), lax.axis_index("c"), lax.axis_index("y"), me]
    ).astype(jnp.int32)
    aligned = shard == HEAD_DIM

    vectors = jnp.stack([ln1_gain, ln1_bias, ln2_gain, ln2_bias], axis=0)
    vectors = jnp.concatenate([vectors, jnp.transpose(qkv_bias)], axis=0).astype(f32).reshape(-1)
    small = jnp.concatenate([vectors, segments.astype(f32), positions.astype(f32)])
    small = lax.all_to_all(
        jnp.broadcast_to(small[None], (devices, small.shape[0])), ALL, 0, 0, tiled=True
    )
    vectors = jnp.transpose(small[:, : 7 * shard].reshape(devices, 7, shard), (1, 0, 2)).reshape(7, width)
    gain_one, shift_one, gain_two, shift_two = (vectors[i][None, :] for i in range(4))
    my_plane = lax.dynamic_slice_in_dim(small[:, 7 * shard :], lax.axis_index("g") * team, team, 0)
    segment_all = my_plane[:, :rows].reshape(packs, seq)
    position_all = my_plane[:, rows:].reshape(packs, seq)
    bias_mine = lax.dynamic_slice_in_dim(
        vectors[4:7].reshape(3, my_heads, team, HEAD_DIM), me, 1, 2
    ).reshape(1, 3 * my_width)

    token_pieces = chip_pieces(tokens)
    qkv_send = after(split_heads(qkv_weight, team), small)
    qkv_mine = plane_all_to_all(qkv_send).reshape(team * shard, 3 * my_width)
    ffn_send = split_ffn([gate_weight, up_weight, down_weight], team, packed)
    ffn_send = after(ffn_send, qkv_mine, *token_pieces)
    ffn_mine = plane_all_to_all(ffn_send).reshape(team * shard, packed)

    frequency = rope_base ** (-jnp.arange(0, ROT_DIMS, 2, dtype=f32) / ROT_DIMS)
    within = jnp.arange(PAIR) % HEAD_DIM
    phases = position_all[:, :, None] * jnp.where(within < ROT_DIMS, frequency[within % (ROT_DIMS // 2)], 0.0)
    cosine = jnp.cos(phases)
    sine = jnp.sin(phases) * jnp.where(within < ROT_DIMS // 2, -1.0, 1.0)
    seg_col, seg_row = segment_all[:, :, None], segment_all[:, None, :]

    def over_g(piece):
        return lax.all_gather(piece, "g", axis=0, tiled=True)

    act_one = norm_rows(token_pieces, gain_one, shift_one)
    ffn_mine = after(ffn_mine, act_one, cosine, sine, seg_col)
    act_one = act_one, swap(act_one, "c")
    if aligned:
        out_rows = after(over_g(o_weight), ffn_mine, act_one[0])
    else:
        out_abs = lax.all_gather(o_weight, ALL, axis=0, tiled=True)
        out_abs = out_abs.reshape(my_heads, team, HEAD_DIM, width)
        out_full = [
            jnp.concatenate(
                [jnp.take(out_abs, slot_of(s, place), axis=1).reshape(my_width, width) for s in span], axis=0
            )
            for span in (range(4), range(4, 8))
        ]
    qkv_full = over_g(qkv_mine)
    ffn_full = over_g(ffn_mine)
    qkv_full = after(qkv_full, act_one[0], ffn_mine)

    qkv, act_one = project(place, act_one, qkv_full, bias_mine, cosine, sine)
    mixed, mixed_halves, totals = attention(place, qkv, blocks, seg_col, seg_row)
    if aligned:
        out_full = halves_of(chip_pieces(out_rows, qkv), mixed)
    hidden, act_two = out_rows_of(
        place, plane_all_to_all(mixed.reshape(team, rows, my_width)), out_full, tokens, gain_two, shift_two
    )

    act_two = halves_of(chip_pieces(act_two))
    cotangent = chip_pieces(after(out_grad, act_two[0]))
    middle_low, by_gate, by_up, act_all = gate_rows(act_two, ffn_full, my_ffn)
    cotangent = halves_of(cotangent, middle_low)
    output_other = plane_send(middle_low, ffn_full, 2 * my_ffn)
    down_sum = row_sum(cotangent, middle_low, kept=my_ffn)
    output_kept = plane_keep(after(middle_low, down_sum), ffn_full, 2 * my_ffn, output_other)

    def own_rows(grad_sum):
        return lax.psum_scatter(grad_sum, "g", scatter_dimension=0, tiled=True)

    def back_to_rows(columns):
        return plane_all_to_all(columns.reshape(team, shard, columns.shape[1]))

    down_own = own_rows(down_sum)
    gate_up_grad = gate_back_rows(after(cotangent, output_kept[0]), ffn_full, by_gate, by_up, my_ffn)
    output_terms = after(plane_corner(output_kept), gate_up_grad)
    norm_two_other = plane_send(after(gate_up_grad, output_terms[0]), ffn_full, 0)
    norm_two_kept = plane_keep(gate_up_grad, ffn_full, 0, norm_two_other, bf16)
    gate_up_sum = row_sum([act_all], after(gate_up_grad, norm_two_kept[0], down_own), time=60)
    output = (hidden + total_of(after(plane_neighbours(output_terms), gate_up_sum))).astype(bf16)
    gate_up_own = own_rows(gate_up_sum)
    norm_two_terms = after(plane_direct(norm_two_kept), output)
    mixed_grad, hidden_grad, hidden_low, two_sums = out_back_rows(
        place, norm_two_terms, hidden, out_grad, gain_two, out_full, time=130
    )
    down_recv = back_to_rows(after(down_own, norm_two_terms))

    mixed_grad = plane_all_to_all(after(mixed_grad, down_recv)).reshape(packs, blocks, rows, my_width)
    qkv_grad = attention_back(place, qkv, mixed_grad, totals, cosine, sine, seg_col, seg_row, time=130)
    qkv_grad = qkv_grad.reshape(8 * rows, 3 * my_width)
    hidden_pieces = chip_pieces(after(hidden_low, mixed_grad), qkv_grad)
    qkv_sum = row_sum([act_one], after(qkv_grad, hidden_pieces[1]), time=130)
    qkv_own = own_rows(qkv_sum)
    norm_one_other = plane_send(after(qkv_grad, qkv_sum, hidden_pieces), qkv_full, 0, time=60)
    hidden_all = halves_of(hidden_pieces, norm_one_other, time=60)
    gate_up_recv = back_to_rows(after(gate_up_own, norm_one_other))
    norm_one_kept = plane_keep(after(qkv_grad, hidden_all[0]), qkv_full, 0, norm_one_other, bf16)
    mixed_halves = mixed_halves.reshape(2, 4 * rows, my_width)
    out_sum = pair_sum(mixed_halves, after(hidden_all, norm_one_kept[0], gate_up_recv), time=60)
    if aligned:
        out_share = own_rows(out_sum).astype(f32)
    else:
        spread = jnp.zeros((my_heads, team, HEAD_DIM, width), bf16)
        spread = lax.dynamic_update_slice_in_dim(
            spread, out_sum.reshape(my_heads, 1, HEAD_DIM, width), me, 1
        )
        out_share = lax.psum_scatter(
            spread.reshape(width, width).astype(f32), ALL, scatter_dimension=0, tiled=True
        )
    norm_one_terms = after(plane_direct(norm_one_kept), out_sum)
    norm_grad_one = total_of(norm_one_terms)
    normed_one, inv_one = layer_stats(tokens.astype(f32))
    input_grad = (hidden_grad + norm_back(norm_grad_one, normed_one, inv_one, gain_one)).astype(bf16)
    down_share = merge_ffn(down_recv, 1, ffn)
    gate_up_share = merge_ffn(gate_up_recv, 2, ffn)

    bias_sum = jnp.sum(qkv_grad.astype(f32), axis=0).reshape(3, my_heads, 1, HEAD_DIM)
    mine = (jnp.arange(team) == me).astype(f32)[None, None, :, None]
    terms = jnp.concatenate(
        [
            jnp.sum(norm_grad_one * normed_one, axis=0)[None],
            jnp.sum(norm_grad_one, axis=0)[None],
            (bias_sum * mine).reshape(3, width),
            two_sums,
        ],
        axis=0,
    )
    qkv_recv = back_to_rows(after(qkv_own, out_sum))
    terms = after(terms, qkv_recv)
    terms = jnp.transpose(terms.reshape(7, devices, shard), (1, 0, 2)).reshape(devices, 7 * shard)
    vector_share = jnp.sum(lax.all_to_all(terms, ALL, 0, 0, tiled=True), axis=0).reshape(7, shard)
    qkv_share = merge_heads(qkv_recv)
    return (
        output,
        input_grad,
        vector_share[0],
        vector_share[1],
        qkv_share,
        jnp.transpose(vector_share[2:5]),
        out_share,
        vector_share[5],
        vector_share[6],
        *gate_up_share,
        *down_share,
    )


def solution(mesh):
    dp, ctx = mesh.shape["dp"], mesh.shape["ctx"]
    split = Mesh(mesh.devices.reshape(dp // 2, 2, ctx // 2, 2), ALL)
    row, flat = P(ALL, None), P(ALL)
    return jax.shard_map(
        local,
        mesh=split,
        in_specs=(row, flat, flat, row, flat, flat, row, row, row, flat, flat, row, row, row),
        out_specs=(row, row, flat, flat, row, row, row, flat, flat, row, row, row),
        check_vma=False,
    )
```

```python
import functools

import jax
import jax.numpy as jnp
from jax import lax
from jax.experimental import pallas as pl
from jax.experimental.pallas import tpu as pltpu
from jax.sharding import Mesh
from jax.sharding import PartitionSpec as P

HEAD_DIM = 64
ROT_DIMS = 16
PAIR = 2 * HEAD_DIM
PLANE = ("y", "x", "c")
ALL = ("g", "y", "x", "c")
bf16 = jnp.bfloat16
f32 = jnp.float32

epsilon = 1e-05
neg_large = -1e30
rope_base = 10000.0
score_scale = 0.125


def layer_stats(values):
    mean_value = jnp.mean(values, axis=-1, keepdims=True)
    centered = values - mean_value
    inv_std = lax.rsqrt(jnp.mean(centered * centered, axis=-1, keepdims=True) + epsilon)
    return (centered * inv_std, inv_std)


def norm_back(grad_rows, normed, inv_std, gain_row):
    scaled = grad_rows * gain_row
    inner = jnp.mean(scaled * normed, axis=-1, keepdims=True)
    return inv_std * (scaled - jnp.mean(scaled, axis=-1, keepdims=True) - normed * inner)


def contract(left, right, left_dim, right_dim, kind=f32):
    return lax.dot_general(
        left, right, (((left_dim,), (right_dim,)), ((), ())), preferred_element_type=f32
    ).astype(kind)


def after(values, *others):
    return lax.optimization_barrier((values, *others))[0]


def fenced(function, *operands):
    shapes = jax.eval_shape(function, *operands)
    return lax.cond(
        lax.axis_index("g") < lax.axis_size("g"),
        function,
        lambda *_: jax.tree.map(lambda leaf: jnp.zeros(leaf.shape, leaf.dtype), shapes),
        *operands,
    )


def swap(values, axis):
    return lax.ppermute(values, axis, [(0, 1), (1, 0)])


def join_kernel(*refs):
    *piece_refs, out_ref = refs
    at = 0
    for piece in piece_refs:
        out_ref[at : at + piece.shape[0], :] = piece[...]
        at += piece.shape[0]


def join(pieces, time=5):
    rows, width = sum(piece.shape[0] for piece in pieces), pieces[0].shape[1]
    return pl.pallas_call(
        join_kernel,
        grid=(4,),
        in_specs=[pl.BlockSpec((piece.shape[0], width // 4), lambda i: (0, i)) for piece in pieces],
        out_specs=pl.BlockSpec((rows, width // 4), lambda i: (0, i)),
        out_shape=jax.ShapeDtypeStruct((rows, width), pieces[0].dtype),
        **limits(time),
    )(*pieces)


def near_pieces(rows):
    return swap(rows, "x"), swap(rows, "y")


def chip_pieces(rows, *first, near=None):
    half = rows.shape[0] // 2
    over_x, over_y = near or near_pieces(rows)
    if first:
        over_x, over_y = lax.optimization_barrier((over_x, over_y, *first))[:2]
    return [rows, over_x, over_y, swap(over_y[:half], "x"), swap(over_x[half:], "y")]


def halves_of(pieces, *first, time=5):
    if first:
        pieces = lax.optimization_barrier((*pieces, *first))[: len(pieces)]
    mine = join(pieces, time)
    return mine, swap(mine, "c")


def send_kernel(left_ref, right_ref, out_ref):
    out_ref[...] = nt(left_ref[...], right_ref[...]).astype(bf16)


def keep_kernel(left_ref, right_ref, other_ref, corner_ref, x_ref, y_ref, own_ref):
    s = pl.program_id(0)
    total = nt(left_ref[...], right_ref[...]) + other_ref[...].astype(f32)

    @pl.when(s == 0)
    def _():
        corner_ref[...] = total.astype(bf16)

    for which, ref in ((1, x_ref), (2, y_ref), (3, own_ref)):

        @pl.when(s == which)
        def _(ref=ref):
            ref[...] = total.astype(ref.dtype)


def corner_first(s):
    return jnp.where(s == 0, 3, jnp.where(s == 3, 0, s))


def columns_of(right, at, depth):
    if right.shape[1] == depth:
        return pl.BlockSpec(right.shape, lambda s: (0, 0))
    return pl.BlockSpec((pl.Element(right.shape[0]), pl.Element(depth)), lambda s: (0, at))


def plane_send(left, right, at, time=None):
    rows, depth, width = left.shape[0] // 8, left.shape[1], right.shape[0]
    return pl.pallas_call(
        send_kernel,
        grid=(2,),
        in_specs=[
            pl.BlockSpec((2 * rows, depth), lambda s: (s + 2, 0)),
            columns_of(right, at, depth),
        ],
        out_specs=pl.BlockSpec((2 * rows, width), lambda s: (s, 0)),
        out_shape=jax.ShapeDtypeStruct((4 * rows, width), bf16),
        **limits(depth // 134 if time is None else time),
    )(left, right)


def plane_keep(left, right, at, other, kind=f32, time=None):
    rows, depth, width = left.shape[0] // 8, left.shape[1], right.shape[0]
    whole = pl.BlockSpec((rows, width), lambda s: (0, 0))
    return pl.pallas_call(
        keep_kernel,
        grid=(4,),
        in_specs=[
            pl.BlockSpec((rows, depth), lambda s: (corner_first(s), 0)),
            columns_of(right, at, depth),
            pl.BlockSpec((rows, width), lambda s: (corner_first(s), 0)),
        ],
        out_specs=[whole] * 4,
        out_shape=[jax.ShapeDtypeStruct((rows, width), kind) for kind in (bf16, kind, kind, f32)],
        **limits(depth // 114 if time is None else time),
    )(left, right, other)


def plane_direct(kept):
    corner, for_x, for_y, own = kept
    far = lax.ppermute(corner, ("y", "x"), [(0, 3), (1, 2), (2, 1), (3, 0)])
    return own, swap(for_x, "x"), swap(for_y, "y"), far


def plane_corner(kept):
    corner, for_x, for_y, own = kept
    half = corner.shape[0] // 2
    from_x = swap(corner[:half], "x")
    from_y = swap(corner[half:], "y")
    to_x = jnp.concatenate([for_x[:half], for_x[half:] + from_y.astype(f32)], axis=0).astype(bf16)
    to_y = jnp.concatenate([for_y[:half] + from_x.astype(f32), for_y[half:]], axis=0).astype(bf16)
    return own, to_x, to_y


def plane_neighbours(terms):
    own, to_x, to_y = terms
    return own, swap(to_x, "x"), swap(to_y, "y")


def total_of(terms):
    return sum(term.astype(f32) for term in terms[1:]) + terms[0]


def sum_kernel(*refs):
    *left_refs, right_ref, out_ref = refs
    total, at = None, 0
    for left_ref in left_refs:
        part = tn(left_ref[...], right_ref[at : at + left_ref.shape[0], :])
        total = part if total is None else total + part
        at += left_ref.shape[0]
    out_ref[...] = total[:, : out_ref.shape[1]].astype(bf16)


def row_sum(left, right, kept=None, time=None):
    width, (rows, columns) = left[0].shape[1], right.shape
    kept = kept or columns
    step = min(width, 512)
    return pl.pallas_call(
        sum_kernel,
        grid=(width // step,),
        in_specs=[
            *[pl.BlockSpec((piece.shape[0], step), lambda i: (0, i)) for piece in left],
            pl.BlockSpec((rows, columns), lambda i: (0, 0)),
        ],
        out_specs=pl.BlockSpec((step, kept), lambda i: (i, 0)),
        out_shape=jax.ShapeDtypeStruct((width, kept), bf16),
        **limits(columns // 83 if time is None else time),
    )(*left, right)


def pair_kernel(left0_ref, left1_ref, right0_ref, right1_ref, out_ref):
    out_ref[...] = (tn(left0_ref[0], right0_ref[...]) + tn(left1_ref[0], right1_ref[...])).astype(bf16)


def pair_sum(left, right, time):
    _, rows, width = left.shape
    columns = right[0].shape[1]
    step = columns // 4
    return pl.pallas_call(
        pair_kernel,
        grid=(4,),
        in_specs=[
            pl.BlockSpec((1, rows, width), lambda i: (0, 0, 0)),
            pl.BlockSpec((1, rows, width), lambda i: (1, 0, 0)),
            pl.BlockSpec((rows, step), lambda i: (0, i)),
            pl.BlockSpec((rows, step), lambda i: (0, i)),
        ],
        out_specs=pl.BlockSpec((width, step), lambda i: (0, i)),
        out_shape=jax.ShapeDtypeStruct((width, columns), bf16),
        **limits(time),
    )(left, left, *right)


def plane_all_to_all(blocks):
    return lax.all_to_all(blocks, PLANE, 0, 0, tiled=True)


def turned(rows, cosine, sine, first):
    partner = jnp.where(first, pltpu.roll(rows, PAIR - ROT_DIMS // 2, 1), pltpu.roll(rows, ROT_DIMS // 2, 1))
    return rows * cosine + partner * sine


def lanes_of(rows):
    return lax.broadcasted_iota(jnp.int32, (rows, PAIR), 1)


def keep_head(values, head):
    lane = lanes_of(values.shape[0])
    inside = lane < HEAD_DIM if head == 0 else lane >= HEAD_DIM
    return jnp.where(inside, values, jnp.zeros_like(values))


def allowed_block(seg_col, seg_row, block, rows):
    same = seg_col[0, : (block + 1) * rows, :] == seg_row[0, :, block * rows : (block + 1) * rows]
    key_at = lax.broadcasted_iota(jnp.int32, same.shape, 0)
    query_at = lax.broadcasted_iota(jnp.int32, same.shape, 1) + block * rows
    return same & (key_at <= query_at)


def where_is(place, block):
    return jnp.bitwise_xor(place[1], block % 2), jnp.bitwise_xor(place[0], block // 2)


def nt(left, right):
    return lax.dot_general(left, right, (((1,), (1,)), ((), ())), preferred_element_type=f32)


def tn(left, right):
    return lax.dot_general(left, right, (((0,), (0,)), ((), ())), preferred_element_type=f32)


def nn(left, right):
    return lax.dot_general(left, right, (((1,), (0,)), ((), ())), preferred_element_type=f32)


def attend_kernel(
    blocks, place, query_ref, key_ref, value_ref, col_ref, row_ref, mixed_ref, halves_ref, total_ref,
):
    rows = mixed_ref.shape[2]
    for block in range(blocks):
        span = slice(block * rows, (block + 1) * rows)
        upto = (block + 1) * rows
        allowed = allowed_block(col_ref, row_ref, block, rows)
        mixed = jnp.zeros((PAIR, rows), f32)
        for head in range(2):
            query = keep_head(query_ref[0, span, :], head) * score_scale
            scores = jnp.where(allowed, nt(key_ref[0, :upto, :], query), neg_large)
            top = jnp.max(scores, axis=0, keepdims=True)
            weights = jnp.exp(scores - top)
            total = jnp.sum(weights, axis=0, keepdims=True)
            probs = (weights * (1.0 / total)).astype(bf16)
            mixed = mixed + tn(keep_head(value_ref[0, :upto, :], head), probs)
            total_ref[0, 0, head : head + 1, span] = top + jnp.log(total)
        mixed = jnp.transpose(mixed).astype(bf16)
        mixed_ref[0, block] = mixed
        half, entry = where_is(place, block)
        halves_ref[half, 0, entry] = mixed


def attend_back_kernel(
    blocks, place, query_ref, key_ref, value_ref, grad_ref, total_ref, cos_ref, sin_ref, col_ref, row_ref,
    out_ref, dk_ref, dv_ref,
):
    pair = pl.program_id(1)
    rows = grad_ref.shape[2]
    width = out_ref.shape[4] // 3
    first = lanes_of(rows) % HEAD_DIM < ROT_DIMS // 2

    def put(block, which, values):
        half, entry = where_is(place, block)
        at = pl.multiple_of(which * width + pair * PAIR, PAIR)
        out_ref[half, 0, entry, :, pl.ds(at, PAIR)] = values.astype(bf16)

    dk_ref[...] = jnp.zeros_like(dk_ref)
    dv_ref[...] = jnp.zeros_like(dv_ref)
    for block in range(blocks):
        span = slice(block * rows, (block + 1) * rows)
        upto = (block + 1) * rows
        allowed = allowed_block(col_ref, row_ref, block, rows)
        dq = jnp.zeros((PAIR, rows), f32)
        for head in range(2):
            query = keep_head(query_ref[0, span, :], head) * score_scale
            grad = keep_head(grad_ref[0, block], head)
            scores = jnp.where(allowed, nt(key_ref[0, :upto, :], query), neg_large)
            probs = jnp.exp(scores - total_ref[0, 0, head : head + 1, span])
            prob_grad = nt(value_ref[0, :upto, :], grad)
            inner = jnp.sum(probs * prob_grad, axis=0, keepdims=True)
            score_grad = (probs * (prob_grad - inner)).astype(bf16)
            dk_ref[:upto, :] += nn(score_grad, query)
            dv_ref[:upto, :] += nn(probs.astype(bf16), grad)
            dq = dq + tn(keep_head(key_ref[0, :upto, :], head), score_grad)
        put(block, 0, turned(jnp.transpose(dq) * score_scale, cos_ref[0, span, :], -sin_ref[0, span, :], first))
    for block in range(blocks):
        span = slice(block * rows, (block + 1) * rows)
        put(block, 1, turned(dk_ref[span, :], cos_ref[0, span, :], -sin_ref[0, span, :], first))
        put(block, 2, dv_ref[span, :])


SHORT = 6


def limits(time):
    return dict(
        compiler_params=pltpu.CompilerParams(vmem_limit_bytes=56 * 1024 * 1024),
        cost_estimate=pl.CostEstimate(flops=time * 10**9 // SHORT, bytes_accessed=time * 3 * 10**6 // SHORT, transcendentals=0),
    )


def qkv_parts(seq, pairs):
    return [
        pl.BlockSpec((1, seq, PAIR), lambda p, h, place, which=which: (p, 0, which * pairs + h))
        for which in range(3)
    ]


def at_pack(*shape):
    rest = (0,) * len(shape)
    return pl.BlockSpec((1, *shape), lambda p, h, place: (jnp.bitwise_xor(p, place[2]), *rest))


def attention(place, qkv, blocks, seg_col, seg_row):
    packs, seq, width = qkv.shape
    width //= 3
    rows, pairs = seq // blocks, width // PAIR
    return pl.pallas_call(
        functools.partial(attend_kernel, blocks),
        grid_spec=pltpu.PrefetchScalarGridSpec(
            num_scalar_prefetch=1,
            grid=(packs, pairs),
            in_specs=[*qkv_parts(seq, pairs), at_pack(seq, 1), at_pack(1, seq)],
            out_specs=[
                pl.BlockSpec(
                    (1, blocks, rows, PAIR), lambda p, h, place: (jnp.bitwise_xor(p, place[2]), 0, 0, h)
                ),
                pl.BlockSpec((2, 1, 2, rows, PAIR), lambda p, h, place: (0, p, 0, 0, h)),
                pl.BlockSpec((1, 1, 2, seq), lambda p, h, place: (p, h, 0, 0)),
            ],
        ),
        out_shape=[
            jax.ShapeDtypeStruct((packs, blocks, rows, width), bf16),
            jax.ShapeDtypeStruct((2, packs, 2, rows, width), bf16),
            jax.ShapeDtypeStruct((packs, pairs, 2, seq), f32),
        ],
        **limits(16),
    )(place, qkv, qkv, qkv, seg_col, seg_row)


def attention_back(place, qkv, grad, totals, cosine, sine, seg_col, seg_row, time=25):
    packs, blocks, rows, width = grad.shape
    pairs, seq = width // PAIR, blocks * rows
    return pl.pallas_call(
        functools.partial(attend_back_kernel, blocks),
        grid_spec=pltpu.PrefetchScalarGridSpec(
            num_scalar_prefetch=1,
            grid=(packs, pairs),
            in_specs=[
                *qkv_parts(seq, pairs),
                pl.BlockSpec(
                    (1, blocks, rows, PAIR), lambda p, h, place: (jnp.bitwise_xor(p, place[2]), 0, 0, h)
                ),
                pl.BlockSpec((1, 1, 2, seq), lambda p, h, place: (p, h, 0, 0)),
                at_pack(seq, PAIR), at_pack(seq, PAIR), at_pack(seq, 1), at_pack(1, seq),
            ],
            out_specs=pl.BlockSpec((2, 1, 2, rows, 3 * width), lambda p, h, place: (0, p, 0, 0, 0)),
            scratch_shapes=[pltpu.VMEM((seq, PAIR), f32)] * 2,
        ),
        out_shape=jax.ShapeDtypeStruct((2, packs, 2, rows, 3 * width), bf16),
        **limits(time),
    )(place, qkv, qkv, qkv, grad, totals, cosine, sine, seg_col, seg_row)


def norm_kernel(*refs):
    *piece_refs, gain_ref, shift_ref, act_ref = refs
    step, at = 64, 0
    for piece in piece_refs:
        for row in range(0, piece.shape[0], step):
            normed = layer_stats(piece[row : row + step, :].astype(f32))[0]
            act_ref[at : at + step, :] = (normed * gain_ref[...] + shift_ref[...]).astype(bf16)
            at += step


def norm_rows(pieces, gain, shift):
    count, width = sum(piece.shape[0] for piece in pieces), gain.shape[1]
    return pl.pallas_call(
        norm_kernel,
        out_shape=jax.ShapeDtypeStruct((count, width), bf16),
        **limits(7),
    )(*pieces, gain, shift)


def pick(halves, steps):
    return jnp.where(pl.program_id(0) < steps // 2, halves[0][...], halves[1][...])


def project_kernel(place, act0_ref, act1_ref, weight_ref, bias_ref, cos_ref, sin_ref, out_ref, act_ref):
    act = pick((act0_ref, act1_ref), 8)
    act_ref[...] = act
    projected = nn(act, weight_ref[...]) + bias_ref[...]
    rows, width = projected.shape
    first = lanes_of(rows) % HEAD_DIM < ROT_DIMS // 2
    cosine, sine = cos_ref[0], sin_ref[0]
    for at in range(0, width, PAIR):
        part = projected[:, at : at + PAIR]
        if at < 2 * width // 3:
            part = turned(part, cosine, sine, first)
        out_ref[0, :, at : at + PAIR] = part.astype(bf16)


def project(place, act, weight, bias, cosine, sine):
    count, depth = act[0].shape
    width = weight.shape[1]
    packs, seq, _ = cosine.shape
    rows = count // 4

    def block_of(s, place):
        return jnp.bitwise_xor(place[0], s % 2) * 2 + jnp.bitwise_xor(place[1], s // 4)

    def table(s, place):
        return (jnp.bitwise_xor(place[2], s // 2 % 2), block_of(s, place), 0)

    return pl.pallas_call(
        project_kernel,
        grid_spec=pltpu.PrefetchScalarGridSpec(
            num_scalar_prefetch=1,
            grid=(8,),
            in_specs=[
                *half_specs(rows, depth),
                pl.BlockSpec((depth, width), lambda s, place: (0, 0)),
                pl.BlockSpec((1, width), lambda s, place: (0, 0)),
                pl.BlockSpec((1, rows, PAIR), table),
                pl.BlockSpec((1, rows, PAIR), table),
            ],
            out_specs=[
                pl.BlockSpec((1, rows, width), lambda s, place: (s // 2 % 2, block_of(s, place), 0)),
                pl.BlockSpec((rows, depth), lambda s, place: (s, 0)),
            ],
        ),
        out_shape=[
            jax.ShapeDtypeStruct((packs, seq, width), bf16), jax.ShapeDtypeStruct((2 * count, depth), bf16)
        ],
        **limits(15),
    )(place, *act, weight, bias, cosine, sine)


def slot_of(s, place):
    return jnp.bitwise_xor(place[3], s // 4 + (s // 2 % 2) * 4 + (s % 2) * 2)


def half_specs(rows, width, steps=8):
    half = steps // 2
    return [
        pl.BlockSpec((rows, width), lambda s, *place: (jnp.minimum(s, half - 1), 0)),
        pl.BlockSpec((rows, width), lambda s, *place: (jnp.maximum(s - half, 0), 0)),
    ]


def out_kernel(place, mixed_ref, w0_ref, w1_ref, token_ref, gain_ref, shift_ref, hidden_ref, act_ref, sum_ref):
    s = pl.program_id(0)

    @pl.when(s == 0)
    def _():
        sum_ref[...] = token_ref[...].astype(f32)

    @pl.when(s < 4)
    def _():
        sum_ref[...] += nn(mixed_ref[0], w0_ref[...])

    @pl.when(s >= 4)
    def _():
        sum_ref[...] += nn(mixed_ref[0], w1_ref[...])

    @pl.when(s == 7)
    def _():
        hidden = sum_ref[...]
        hidden_ref[...] = hidden
        act_ref[...] = (layer_stats(hidden)[0] * gain_ref[...] + shift_ref[...]).astype(bf16)


def out_rows_of(place, mixed, weight, tokens, gain, shift):
    rows, width = tokens.shape
    part = mixed.shape[2]
    whole = pl.BlockSpec((rows, width), lambda s, place: (0, 0))
    vector = pl.BlockSpec((1, width), lambda s, place: (0, 0))
    return pl.pallas_call(
        out_kernel,
        grid_spec=pltpu.PrefetchScalarGridSpec(
            num_scalar_prefetch=1,
            grid=(8,),
            in_specs=[
                pl.BlockSpec((1, rows, part), lambda s, place: (slot_of(s, place), 0, 0)),
                *half_specs(part, width), whole, vector, vector,
            ],
            out_specs=[whole, whole],
            scratch_shapes=[pltpu.VMEM((rows, width), f32)],
        ),
        out_shape=[jax.ShapeDtypeStruct((rows, width), f32), jax.ShapeDtypeStruct((rows, width), bf16)],
        **limits(12),
    )(place, mixed, *weight, tokens, gain, shift)


def out_back_kernel(
    place, own_ref, x_ref, y_ref, far_ref, hidden_ref, grad_ref, gain_ref, w0_ref, w1_ref,
    mixed_ref, total_ref, low_ref, vector_ref,
):
    s = pl.program_id(0)

    @pl.when(s == 0)
    def _():
        norm_grad = own_ref[...] + x_ref[...].astype(f32) + y_ref[...].astype(f32) + far_ref[...].astype(f32)
        normed, inv_std = layer_stats(hidden_ref[...])
        vector_ref[0:1, :] = jnp.sum(norm_grad * normed, axis=0, keepdims=True)
        vector_ref[1:2, :] = jnp.sum(norm_grad, axis=0, keepdims=True)
        total = grad_ref[...].astype(f32) + norm_back(norm_grad, normed, inv_std, gain_ref[...])
        total_ref[...] = total
        low_ref[...] = total.astype(bf16)

    @pl.when(s < 4)
    def _():
        mixed_ref[0] = nt(low_ref[...], w0_ref[...]).astype(bf16)

    @pl.when(s >= 4)
    def _():
        mixed_ref[0] = nt(low_ref[...], w1_ref[...]).astype(bf16)


def out_back_rows(place, terms, hidden, out_grad, gain, weight, time=15):
    rows, width = hidden.shape
    part = weight[0].shape[0] // 4
    whole = pl.BlockSpec((rows, width), lambda s, place: (0, 0))
    vector = pl.BlockSpec((1, width), lambda s, place: (0, 0))
    return pl.pallas_call(
        out_back_kernel,
        grid_spec=pltpu.PrefetchScalarGridSpec(
            num_scalar_prefetch=1,
            grid=(8,),
            in_specs=[*[whole] * 6, vector, *half_specs(part, width)],
            out_specs=[
                pl.BlockSpec((1, rows, part), lambda s, place: (slot_of(s, place), 0, 0)),
                whole, whole, pl.BlockSpec((2, width), lambda s, place: (0, 0)),
            ],
        ),
        out_shape=[
            jax.ShapeDtypeStruct((8, rows, part), bf16),
            jax.ShapeDtypeStruct((rows, width), f32),
            jax.ShapeDtypeStruct((rows, width), bf16),
            jax.ShapeDtypeStruct((2, width), f32),
        ],
        **limits(time),
    )(place, *terms, hidden, out_grad, gain, *weight)


STEPS = 4


def gate_kernel(act0_ref, act1_ref, weight_ref, middle_ref, by_gate_ref, by_up_ref, act_ref):
    act = pick((act0_ref, act1_ref), STEPS)
    act_ref[...] = act
    both = nn(act, weight_ref[...])
    half, wide = both.shape[1] // 2, middle_ref.shape[1]
    inside = lax.broadcasted_iota(jnp.int32, (both.shape[0], wide), 1) < half
    gate = jnp.where(inside, both[:, :wide], 0.0)
    up = jnp.where(inside, pltpu.roll(both[:, 2 * half - wide :], half, 1), 0.0)
    sigmoid = jax.nn.sigmoid(gate)
    silu = gate * sigmoid
    middle_ref[...] = (silu * up).astype(bf16)
    by_gate_ref[...] = (up * (sigmoid * (1.0 + gate * (1.0 - sigmoid)))).astype(bf16)
    by_up_ref[...] = silu.astype(bf16)


def gate_rows(act, weight, half):
    count, depth = act[0].shape
    count *= 2
    wide, rows = -(-half // PAIR) * PAIR, count // STEPS
    out = pl.BlockSpec((rows, wide), lambda s: (s, 0))
    return pl.pallas_call(
        gate_kernel,
        grid=(STEPS,),
        in_specs=[*half_specs(rows, depth, STEPS), pl.BlockSpec((depth, 2 * half), lambda s: (0, 0))],
        out_specs=[out] * 3 + [pl.BlockSpec((rows, depth), lambda s: (s, 0))],
        out_shape=[jax.ShapeDtypeStruct((count, wide), bf16)] * 3 + [jax.ShapeDtypeStruct((count, depth), bf16)],
        **limits(20),
    )(*act, weight)


def gate_back_kernel(grad0_ref, grad1_ref, weight_ref, by_gate_ref, by_up_ref, out_ref):
    middle = nn(pick((grad0_ref, grad1_ref), STEPS), weight_ref[...])
    gate = middle * by_gate_ref[...].astype(f32)
    half, wide = out_ref.shape[1] // 2, middle.shape[1]
    up = pltpu.roll(middle * by_up_ref[...].astype(f32), half - (2 * half - wide), 1)
    cut = 2 * half - wide
    out_ref[:, :cut] = gate[:, :cut].astype(bf16)
    out_ref[:, cut:wide] = (gate[:, cut:] + up[:, : wide - cut]).astype(bf16)
    out_ref[:, wide:] = up[:, wide - cut :].astype(bf16)


def gate_back_rows(grad, weight, by_gate, by_up, half):
    count, depth = grad[0].shape
    count *= 2
    wide, rows = by_gate.shape[1], count // STEPS
    part = pl.BlockSpec((rows, wide), lambda s: (s, 0))
    return pl.pallas_call(
        gate_back_kernel,
        grid=(STEPS,),
        in_specs=[
            *half_specs(rows, depth, STEPS), columns_of(weight, 2 * half, wide), part, part
        ],
        out_specs=pl.BlockSpec((rows, 2 * half), lambda s: (s, 0)),
        out_shape=jax.ShapeDtypeStruct((count, 2 * half), bf16),
        **limits(13),
    )(*grad, weight, by_gate, by_up)


def halves(low_part, low_at, high_part, high_at):
    low_part = low_part if low_at == 0 else pltpu.roll(low_part, HEAD_DIM, 1)
    high_part = high_part if high_at else pltpu.roll(high_part, HEAD_DIM, 1)
    return jnp.where(lanes_of(low_part.shape[0]) < HEAD_DIM, low_part, high_part)


def lane_group(load, at):
    return load(at // PAIR * PAIR), at % PAIR


def split_heads_kernel(team, weight_ref, out_ref):
    def load(at):
        return weight_ref[:, at : at + PAIR].astype(f32)

    chunks = weight_ref.shape[1] // (team * HEAD_DIM)
    for p in range(team):
        for chunk in range(0, chunks, 2):
            low = lane_group(load, (chunk * team + p) * HEAD_DIM)
            high = lane_group(load, ((chunk + 1) * team + p) * HEAD_DIM)
            out_ref[p, :, chunk * HEAD_DIM : (chunk + 2) * HEAD_DIM] = halves(*low, *high).astype(bf16)


def split_heads(weight, team):
    rows, width = weight.shape
    return pl.pallas_call(
        functools.partial(split_heads_kernel, team),
        out_shape=jax.ShapeDtypeStruct((team, rows, width // team), bf16),
        **limits(2),
    )(weight)


def merge_heads_kernel(part_ref, out_ref):
    team = part_ref.shape[0]
    chunks = part_ref.shape[2] // HEAD_DIM
    for chunk in range(chunks):
        for p in range(0, team, 2):
            at = chunk * HEAD_DIM

            def load(at, p=p):
                return part_ref[p, :, at : at + PAIR].astype(f32)

            def load_next(at, p=p):
                return part_ref[p + 1, :, at : at + PAIR].astype(f32)

            to = (chunk * team + p) * HEAD_DIM
            out_ref[:, to : to + PAIR] = halves(*lane_group(load, at), *lane_group(load_next, at))


def merge_heads(parts):
    team, rows, width = parts.shape
    return pl.pallas_call(
        merge_heads_kernel,
        out_shape=jax.ShapeDtypeStruct((rows, team * width), f32),
        **limits(2),
    )(parts)


def split_ffn_kernel(team, my_ffn, *refs):
    *weight_refs, out_ref = refs
    steps = my_ffn // HEAD_DIM

    def chunk(p, at):
        which, inside = at // steps, at % steps * HEAD_DIM
        if which == len(weight_refs):
            return jnp.zeros((out_ref.shape[1], PAIR), f32), at % 2 * HEAD_DIM
        return lane_group(
            lambda lane: weight_refs[which][:, lane : lane + PAIR].astype(f32), p * my_ffn + inside
        )

    for p in range(team):
        for at in range(0, out_ref.shape[2], PAIR):
            first = at // HEAD_DIM
            out_ref[p, :, at : at + PAIR] = halves(*chunk(p, first), *chunk(p, first + 1)).astype(bf16)


def split_ffn(weights, team, packed):
    rows, width = weights[0].shape
    return pl.pallas_call(
        functools.partial(split_ffn_kernel, team, width // team),
        out_shape=jax.ShapeDtypeStruct((team, rows, packed), bf16),
        **limits(3),
    )(*weights)


def merge_ffn_kernel(my_ffn, part_ref, *out_refs):
    team = part_ref.shape[0]
    for which, out_ref in enumerate(out_refs):

        def chunk(at):
            p, inside = at // my_ffn, at % my_ffn
            group, lane = (which * my_ffn + inside) // PAIR * PAIR, (which * my_ffn + inside) % PAIR
            return part_ref[p, :, group : group + PAIR].astype(f32), lane

        for at in range(0, team * my_ffn, PAIR):
            out_ref[:, at : at + PAIR] = halves(*chunk(at), *chunk(at + HEAD_DIM))


def merge_ffn(parts, count, ffn):
    team, rows, width = parts.shape
    parts = jnp.pad(parts, ((0, 0), (0, 0), (0, -width % PAIR)))
    return pl.pallas_call(
        functools.partial(merge_ffn_kernel, ffn // team),
        out_shape=[jax.ShapeDtypeStruct((rows, ffn), f32)] * count,
        **limits(3),
    )(parts)


def local(
    tokens, segments, positions, out_grad, ln1_gain, ln1_bias, qkv_weight, qkv_bias, o_weight,
    ln2_gain, ln2_bias, gate_weight, up_weight, down_weight,
):
    rows, width = tokens.shape
    shard = qkv_weight.shape[0]
    ffn = gate_weight.shape[1]
    heads = width // HEAD_DIM
    team = lax.axis_size(PLANE)
    depth = lax.axis_size("g")
    devices = team * depth
    packs = lax.axis_size("y")
    blocks = team // packs
    seq = blocks * rows
    my_heads = heads // team
    my_width = my_heads * HEAD_DIM
    my_ffn = ffn // team
    packed = -(-3 * my_ffn // PAIR) * PAIR
    me = lax.axis_index(PLANE)
    place = jnp.stack(
        [lax.axis_index("x"), lax.axis_index("c"), lax.axis_index("y"), me]
    ).astype(jnp.int32)
    aligned = shard == HEAD_DIM

    vectors = jnp.stack([ln1_gain, ln1_bias, ln2_gain, ln2_bias], axis=0)
    vectors = jnp.concatenate([vectors, jnp.transpose(qkv_bias)], axis=0).astype(f32).reshape(-1)
    small = jnp.concatenate([vectors, segments.astype(f32), positions.astype(f32)])
    small = lax.all_to_all(
        jnp.broadcast_to(small[None], (devices, small.shape[0])), ALL, 0, 0, tiled=True
    )
    vectors = jnp.transpose(small[:, : 7 * shard].reshape(devices, 7, shard), (1, 0, 2)).reshape(7, width)
    gain_one, shift_one, gain_two, shift_two = (vectors[i][None, :] for i in range(4))
    my_plane = lax.dynamic_slice_in_dim(small[:, 7 * shard :], lax.axis_index("g") * team, team, 0)
    segment_all = my_plane[:, :rows].reshape(packs, seq)
    position_all = my_plane[:, rows:].reshape(packs, seq)
    bias_mine = lax.dynamic_slice_in_dim(
        vectors[4:7].reshape(3, my_heads, team, HEAD_DIM), me, 1, 2
    ).reshape(1, 3 * my_width)

    token_pieces = chip_pieces(tokens)
    qkv_send = after(split_heads(qkv_weight, team), small)
    qkv_mine = plane_all_to_all(qkv_send).reshape(team * shard, 3 * my_width)
    ffn_send = split_ffn([gate_weight, up_weight, down_weight], team, packed)
    ffn_send = after(ffn_send, qkv_mine, *token_pieces)
    ffn_mine = plane_all_to_all(ffn_send).reshape(team * shard, packed)

    frequency = rope_base ** (-jnp.arange(0, ROT_DIMS, 2, dtype=f32) / ROT_DIMS)
    within = jnp.arange(PAIR) % HEAD_DIM
    phases = position_all[:, :, None] * jnp.where(within < ROT_DIMS, frequency[within % (ROT_DIMS // 2)], 0.0)
    cosine = jnp.cos(phases)
    sine = jnp.sin(phases) * jnp.where(within < ROT_DIMS // 2, -1.0, 1.0)
    seg_col, seg_row = segment_all[:, :, None], segment_all[:, None, :]

    def over_g(piece):
        return lax.all_gather(piece, "g", axis=0, tiled=True)

    act_one = norm_rows(token_pieces, gain_one, shift_one)
    ffn_mine = after(ffn_mine, act_one, cosine, sine, seg_col)
    act_one = act_one, swap(act_one, "c")
    if aligned:
        out_rows = after(over_g(o_weight), ffn_mine, act_one[0])
    else:
        out_abs = lax.all_gather(o_weight, ALL, axis=0, tiled=True)
        out_abs = out_abs.reshape(my_heads, team, HEAD_DIM, width)
        out_full = [
            jnp.concatenate(
                [jnp.take(out_abs, slot_of(s, place), axis=1).reshape(my_width, width) for s in span], axis=0
            )
            for span in (range(4), range(4, 8))
        ]
    qkv_full = over_g(qkv_mine)
    ffn_full = over_g(ffn_mine)
    qkv_full = after(qkv_full, act_one[0], ffn_mine)

    qkv, act_one = project(place, act_one, qkv_full, bias_mine, cosine, sine)
    mixed, mixed_halves, totals = attention(place, qkv, blocks, seg_col, seg_row)
    if aligned:
        out_full = halves_of(chip_pieces(out_rows, qkv), mixed)
    hidden, act_two = out_rows_of(
        place, plane_all_to_all(mixed.reshape(team, rows, my_width)), out_full, tokens, gain_two, shift_two
    )

    act_two = halves_of(chip_pieces(act_two))
    cotangent = chip_pieces(after(out_grad, act_two[0]))
    middle_low, by_gate, by_up, act_all = gate_rows(act_two, ffn_full, my_ffn)
    cotangent = halves_of(cotangent, middle_low)
    output_other = swap(plane_send(middle_low, ffn_full, 2 * my_ffn), "c")
    down_sum = row_sum(cotangent, middle_low, kept=my_ffn)
    output_kept = plane_keep(after(middle_low, down_sum), ffn_full, 2 * my_ffn, output_other)

    def own_rows(grad_sum):
        return lax.psum_scatter(grad_sum, "g", scatter_dimension=0, tiled=True)

    def back_to_rows(columns):
        return plane_all_to_all(columns.reshape(team, shard, columns.shape[1]))

    down_own = own_rows(down_sum)
    gate_up_grad = gate_back_rows(after(cotangent, output_kept[0]), ffn_full, by_gate, by_up, my_ffn)
    output_terms = after(plane_corner(output_kept), gate_up_grad)
    norm_two_other = swap(plane_send(after(gate_up_grad, output_terms[0]), ffn_full, 0), "c")
    norm_two_kept = plane_keep(gate_up_grad, ffn_full, 0, norm_two_other, bf16)
    gate_up_sum = row_sum([act_all], after(gate_up_grad, norm_two_kept[0], down_own), time=60)
    output = (hidden + total_of(after(plane_neighbours(output_terms), gate_up_sum))).astype(bf16)
    gate_up_own = own_rows(gate_up_sum)
    norm_two_terms = after(plane_direct(norm_two_kept), output)
    mixed_grad, hidden_grad, hidden_low, two_sums = out_back_rows(
        place, norm_two_terms, hidden, out_grad, gain_two, out_full, time=130
    )
    down_recv = back_to_rows(after(down_own, norm_two_terms))

    mixed_grad = plane_all_to_all(after(mixed_grad, down_recv)).reshape(packs, blocks, rows, my_width)
    qkv_grad = attention_back(place, qkv, mixed_grad, totals, cosine, sine, seg_col, seg_row, time=130)
    qkv_grad = qkv_grad.reshape(8 * rows, 3 * my_width)
    hidden_pieces = chip_pieces(after(hidden_low, mixed_grad), qkv_grad)
    qkv_sum = row_sum([act_one], after(qkv_grad, hidden_pieces[1]), time=130)
    qkv_own = own_rows(qkv_sum)
    norm_one_sent = plane_send(after(qkv_grad, qkv_sum, hidden_pieces), qkv_full, 0, time=60)
    norm_one_other = swap(norm_one_sent, "c")
    hidden_all = halves_of(hidden_pieces, norm_one_other, time=60)
    gate_up_recv = back_to_rows(after(gate_up_own, norm_one_other))
    norm_one_kept = plane_keep(after(qkv_grad, hidden_all[0]), qkv_full, 0, norm_one_other, bf16)
    mixed_halves = mixed_halves.reshape(2, 4 * rows, my_width)
    out_sum = pair_sum(mixed_halves, after(hidden_all, norm_one_kept[0], gate_up_recv), time=60)
    if aligned:
        out_share = own_rows(out_sum).astype(f32)
    else:
        spread = jnp.zeros((my_heads, team, HEAD_DIM, width), bf16)
        spread = lax.dynamic_update_slice_in_dim(
            spread, out_sum.reshape(my_heads, 1, HEAD_DIM, width), me, 1
        )
        out_share = lax.psum_scatter(
            spread.reshape(width, width).astype(f32), ALL, scatter_dimension=0, tiled=True
        )
    norm_one_terms = after(plane_direct(norm_one_kept), out_sum)
    qkv_recv = back_to_rows(after(qkv_own, out_sum))
    norm_grad_one = total_of(after(norm_one_terms, qkv_recv))
    normed_one, inv_one = layer_stats(tokens.astype(f32))
    input_grad = (hidden_grad + norm_back(norm_grad_one, normed_one, inv_one, gain_one)).astype(bf16)
    down_share = merge_ffn(after(down_recv, out_sum), 1, ffn)
    gate_up_share = merge_ffn(gate_up_recv, 2, ffn)

    bias_sum = jnp.sum(qkv_grad.astype(f32), axis=0).reshape(3, my_heads, 1, HEAD_DIM)
    mine = (jnp.arange(team) == me).astype(f32)[None, None, :, None]
    terms = jnp.concatenate(
        [
            jnp.sum(norm_grad_one * normed_one, axis=0)[None],
            jnp.sum(norm_grad_one, axis=0)[None],
            (bias_sum * mine).reshape(3, width),
            two_sums,
        ],
        axis=0,
    )
    terms = jnp.transpose(terms.reshape(7, devices, shard), (1, 0, 2)).reshape(devices, 7 * shard)
    vector_share = jnp.sum(lax.all_to_all(terms, ALL, 0, 0, tiled=True), axis=0).reshape(7, shard)
    qkv_share = merge_heads(qkv_recv)
    return (
        output,
        input_grad,
        vector_share[0],
        vector_share[1],
        qkv_share,
        jnp.transpose(vector_share[2:5]),
        out_share,
        vector_share[5],
        vector_share[6],
        *gate_up_share,
        *down_share,
    )


def solution(mesh):
    dp, ctx = mesh.shape["dp"], mesh.shape["ctx"]
    split = Mesh(mesh.devices.reshape(dp // 2, 2, ctx // 2, 2), ALL)
    row, flat = P(ALL, None), P(ALL)
    return jax.shard_map(
        local,
        mesh=split,
        in_specs=(row, flat, flat, row, flat, flat, row, row, row, flat, flat, row, row, row),
        out_specs=(row, row, flat, flat, row, row, row, flat, flat, row, row, row),
        check_vma=False,
    )
```

```python
import functools

import jax
import jax.numpy as jnp
from jax import lax
from jax.experimental import pallas as pl
from jax.experimental.pallas import tpu as pltpu
from jax.sharding import Mesh
from jax.sharding import PartitionSpec as P

HEAD_DIM = 64
ROT_DIMS = 16
PAIR = 2 * HEAD_DIM
PLANE = ("y", "x", "c")
ALL = ("g", "y", "x", "c")
bf16 = jnp.bfloat16
f32 = jnp.float32

epsilon = 1e-05
neg_large = -1e30
rope_base = 10000.0
score_scale = 0.125


def layer_stats(values):
    mean_value = jnp.mean(values, axis=-1, keepdims=True)
    centered = values - mean_value
    inv_std = lax.rsqrt(jnp.mean(centered * centered, axis=-1, keepdims=True) + epsilon)
    return (centered * inv_std, inv_std)


def norm_back(grad_rows, normed, inv_std, gain_row):
    scaled = grad_rows * gain_row
    inner = jnp.mean(scaled * normed, axis=-1, keepdims=True)
    return inv_std * (scaled - jnp.mean(scaled, axis=-1, keepdims=True) - normed * inner)


def contract(left, right, left_dim, right_dim, kind=f32):
    return lax.dot_general(
        left, right, (((left_dim,), (right_dim,)), ((), ())), preferred_element_type=f32
    ).astype(kind)


def after(values, *others):
    return lax.optimization_barrier((values, *others))[0]


def fenced(function, *operands):
    shapes = jax.eval_shape(function, *operands)
    return lax.cond(
        lax.axis_index("g") < lax.axis_size("g"),
        function,
        lambda *_: jax.tree.map(lambda leaf: jnp.zeros(leaf.shape, leaf.dtype), shapes),
        *operands,
    )


def swap(values, axis):
    return lax.ppermute(values, axis, [(0, 1), (1, 0)])


def join_kernel(*refs):
    *piece_refs, out_ref = refs
    at = 0
    for piece in piece_refs:
        out_ref[at : at + piece.shape[0], :] = piece[...]
        at += piece.shape[0]


def join(pieces, time=5):
    rows, width = sum(piece.shape[0] for piece in pieces), pieces[0].shape[1]
    return pl.pallas_call(
        join_kernel,
        grid=(4,),
        in_specs=[pl.BlockSpec((piece.shape[0], width // 4), lambda i: (0, i)) for piece in pieces],
        out_specs=pl.BlockSpec((rows, width // 4), lambda i: (0, i)),
        out_shape=jax.ShapeDtypeStruct((rows, width), pieces[0].dtype),
        **limits(time),
    )(*pieces)


def near_pieces(rows):
    return swap(rows, "x"), swap(rows, "y")


def chip_pieces(rows, *first, near=None):
    half = rows.shape[0] // 2
    over_x, over_y = near or near_pieces(rows)
    if first:
        over_x, over_y = lax.optimization_barrier((over_x, over_y, *first))[:2]
    return [rows, over_x, over_y, swap(over_y[:half], "x"), swap(over_x[half:], "y")]


def halves_of(pieces, *first, time=5):
    if first:
        pieces = lax.optimization_barrier((*pieces, *first))[: len(pieces)]
    mine = join(pieces, time)
    return mine, swap(mine, "c")


def send_kernel(left_ref, right_ref, out_ref):
    out_ref[...] = nt(left_ref[...], right_ref[...]).astype(bf16)


def keep_kernel(left_ref, right_ref, other_ref, corner_ref, x_ref, y_ref, own_ref):
    s = pl.program_id(0)
    total = nt(left_ref[...], right_ref[...]) + other_ref[...].astype(f32)

    @pl.when(s == 0)
    def _():
        corner_ref[...] = total.astype(bf16)

    for which, ref in ((1, x_ref), (2, y_ref), (3, own_ref)):

        @pl.when(s == which)
        def _(ref=ref):
            ref[...] = total.astype(ref.dtype)


def corner_first(s):
    return jnp.where(s == 0, 3, jnp.where(s == 3, 0, s))


def columns_of(right, at, depth):
    if right.shape[1] == depth:
        return pl.BlockSpec(right.shape, lambda s: (0, 0))
    return pl.BlockSpec((pl.Element(right.shape[0]), pl.Element(depth)), lambda s: (0, at))


def plane_send(left, right, at, time=None):
    rows, depth, width = left.shape[0] // 8, left.shape[1], right.shape[0]
    return pl.pallas_call(
        send_kernel,
        grid=(2,),
        in_specs=[
            pl.BlockSpec((2 * rows, depth), lambda s: (s + 2, 0)),
            columns_of(right, at, depth),
        ],
        out_specs=pl.BlockSpec((2 * rows, width), lambda s: (s, 0)),
        out_shape=jax.ShapeDtypeStruct((4 * rows, width), bf16),
        **limits(depth // 134 if time is None else time),
    )(left, right)


def plane_keep(left, right, at, other, kind=f32, time=None):
    rows, depth, width = left.shape[0] // 8, left.shape[1], right.shape[0]
    whole = pl.BlockSpec((rows, width), lambda s: (0, 0))
    return pl.pallas_call(
        keep_kernel,
        grid=(4,),
        in_specs=[
            pl.BlockSpec((rows, depth), lambda s: (corner_first(s), 0)),
            columns_of(right, at, depth),
            pl.BlockSpec((rows, width), lambda s: (corner_first(s), 0)),
        ],
        out_specs=[whole] * 4,
        out_shape=[jax.ShapeDtypeStruct((rows, width), kind) for kind in (bf16, kind, kind, f32)],
        **limits(depth // 114 if time is None else time),
    )(left, right, other)


def plane_direct(kept):
    corner, for_x, for_y, own = kept
    far = lax.ppermute(corner, ("y", "x"), [(0, 3), (1, 2), (2, 1), (3, 0)])
    return own, swap(for_x, "x"), swap(for_y, "y"), far


def plane_corner(kept):
    corner, for_x, for_y, own = kept
    half = corner.shape[0] // 2
    from_x = swap(corner[:half], "x")
    from_y = swap(corner[half:], "y")
    to_x = jnp.concatenate([for_x[:half], for_x[half:] + from_y.astype(f32)], axis=0).astype(bf16)
    to_y = jnp.concatenate([for_y[:half] + from_x.astype(f32), for_y[half:]], axis=0).astype(bf16)
    return own, to_x, to_y


def plane_neighbours(terms):
    own, to_x, to_y = terms
    return own, swap(to_x, "x"), swap(to_y, "y")


def total_of(terms):
    return sum(term.astype(f32) for term in terms[1:]) + terms[0]


def sum_kernel(*refs):
    *left_refs, right_ref, out_ref = refs
    total, at = None, 0
    for left_ref in left_refs:
        part = tn(left_ref[...], right_ref[at : at + left_ref.shape[0], :])
        total = part if total is None else total + part
        at += left_ref.shape[0]
    out_ref[...] = total[:, : out_ref.shape[1]].astype(bf16)


def row_sum(left, right, kept=None, time=None):
    width, (rows, columns) = left[0].shape[1], right.shape
    kept = kept or columns
    step = min(width, 512)
    return pl.pallas_call(
        sum_kernel,
        grid=(width // step,),
        in_specs=[
            *[pl.BlockSpec((piece.shape[0], step), lambda i: (0, i)) for piece in left],
            pl.BlockSpec((rows, columns), lambda i: (0, 0)),
        ],
        out_specs=pl.BlockSpec((step, kept), lambda i: (i, 0)),
        out_shape=jax.ShapeDtypeStruct((width, kept), bf16),
        **limits(columns // 83 if time is None else time),
    )(*left, right)


def pair_kernel(left0_ref, left1_ref, right0_ref, right1_ref, out_ref):
    out_ref[...] = (tn(left0_ref[0], right0_ref[...]) + tn(left1_ref[0], right1_ref[...])).astype(bf16)


def pair_sum(left, right, time):
    _, rows, width = left.shape
    columns = right[0].shape[1]
    step = columns // 4
    return pl.pallas_call(
        pair_kernel,
        grid=(4,),
        in_specs=[
            pl.BlockSpec((1, rows, width), lambda i: (0, 0, 0)),
            pl.BlockSpec((1, rows, width), lambda i: (1, 0, 0)),
            pl.BlockSpec((rows, step), lambda i: (0, i)),
            pl.BlockSpec((rows, step), lambda i: (0, i)),
        ],
        out_specs=pl.BlockSpec((width, step), lambda i: (0, i)),
        out_shape=jax.ShapeDtypeStruct((width, columns), bf16),
        **limits(time),
    )(left, left, *right)


def plane_all_to_all(blocks):
    return lax.all_to_all(blocks, PLANE, 0, 0, tiled=True)


def turned(rows, cosine, sine, first):
    partner = jnp.where(first, pltpu.roll(rows, PAIR - ROT_DIMS // 2, 1), pltpu.roll(rows, ROT_DIMS // 2, 1))
    return rows * cosine + partner * sine


def lanes_of(rows):
    return lax.broadcasted_iota(jnp.int32, (rows, PAIR), 1)


def keep_head(values, head):
    lane = lanes_of(values.shape[0])
    inside = lane < HEAD_DIM if head == 0 else lane >= HEAD_DIM
    return jnp.where(inside, values, jnp.zeros_like(values))


def allowed_block(seg_col, seg_row, block, rows):
    same = seg_col[0, : (block + 1) * rows, :] == seg_row[0, :, block * rows : (block + 1) * rows]
    key_at = lax.broadcasted_iota(jnp.int32, same.shape, 0)
    query_at = lax.broadcasted_iota(jnp.int32, same.shape, 1) + block * rows
    return same & (key_at <= query_at)


def where_is(place, block):
    return jnp.bitwise_xor(place[1], block % 2), jnp.bitwise_xor(place[0], block // 2)


def nt(left, right):
    return lax.dot_general(left, right, (((1,), (1,)), ((), ())), preferred_element_type=f32)


def tn(left, right):
    return lax.dot_general(left, right, (((0,), (0,)), ((), ())), preferred_element_type=f32)


def nn(left, right):
    return lax.dot_general(left, right, (((1,), (0,)), ((), ())), preferred_element_type=f32)


def attend_kernel(
    blocks, place, query_ref, key_ref, value_ref, col_ref, row_ref, mixed_ref, halves_ref, total_ref,
):
    rows = mixed_ref.shape[2]
    for block in range(blocks):
        span = slice(block * rows, (block + 1) * rows)
        upto = (block + 1) * rows
        allowed = allowed_block(col_ref, row_ref, block, rows)
        mixed = jnp.zeros((PAIR, rows), f32)
        for head in range(2):
            query = keep_head(query_ref[0, span, :], head) * score_scale
            scores = jnp.where(allowed, nt(key_ref[0, :upto, :], query), neg_large)
            top = jnp.max(scores, axis=0, keepdims=True)
            weights = jnp.exp(scores - top)
            total = jnp.sum(weights, axis=0, keepdims=True)
            probs = (weights * (1.0 / total)).astype(bf16)
            mixed = mixed + tn(keep_head(value_ref[0, :upto, :], head), probs)
            total_ref[0, 0, head : head + 1, span] = top + jnp.log(total)
        mixed = jnp.transpose(mixed).astype(bf16)
        mixed_ref[0, block] = mixed
        half, entry = where_is(place, block)
        halves_ref[half, 0, entry] = mixed


def attend_back_kernel(
    blocks, place, query_ref, key_ref, value_ref, grad_ref, total_ref, cos_ref, sin_ref, col_ref, row_ref,
    out_ref, dk_ref, dv_ref,
):
    pair = pl.program_id(1)
    rows = grad_ref.shape[2]
    width = out_ref.shape[4] // 3
    first = lanes_of(rows) % HEAD_DIM < ROT_DIMS // 2

    def put(block, which, values):
        half, entry = where_is(place, block)
        at = pl.multiple_of(which * width + pair * PAIR, PAIR)
        out_ref[half, 0, entry, :, pl.ds(at, PAIR)] = values.astype(bf16)

    dk_ref[...] = jnp.zeros_like(dk_ref)
    dv_ref[...] = jnp.zeros_like(dv_ref)
    for block in range(blocks):
        span = slice(block * rows, (block + 1) * rows)
        upto = (block + 1) * rows
        allowed = allowed_block(col_ref, row_ref, block, rows)
        dq = jnp.zeros((PAIR, rows), f32)
        for head in range(2):
            query = keep_head(query_ref[0, span, :], head) * score_scale
            grad = keep_head(grad_ref[0, block], head)
            scores = jnp.where(allowed, nt(key_ref[0, :upto, :], query), neg_large)
            probs = jnp.exp(scores - total_ref[0, 0, head : head + 1, span])
            prob_grad = nt(value_ref[0, :upto, :], grad)
            inner = jnp.sum(probs * prob_grad, axis=0, keepdims=True)
            score_grad = (probs * (prob_grad - inner)).astype(bf16)
            dk_ref[:upto, :] += nn(score_grad, query)
            dv_ref[:upto, :] += nn(probs.astype(bf16), grad)
            dq = dq + tn(keep_head(key_ref[0, :upto, :], head), score_grad)
        put(block, 0, turned(jnp.transpose(dq) * score_scale, cos_ref[0, span, :], -sin_ref[0, span, :], first))
    for block in range(blocks):
        span = slice(block * rows, (block + 1) * rows)
        put(block, 1, turned(dk_ref[span, :], cos_ref[0, span, :], -sin_ref[0, span, :], first))
        put(block, 2, dv_ref[span, :])


SHORT = 6


def limits(time):
    return dict(
        compiler_params=pltpu.CompilerParams(vmem_limit_bytes=56 * 1024 * 1024),
        cost_estimate=pl.CostEstimate(flops=time * 10**9 // SHORT, bytes_accessed=time * 3 * 10**6 // SHORT, transcendentals=0),
    )


def qkv_parts(seq, pairs):
    return [
        pl.BlockSpec((1, seq, PAIR), lambda p, h, place, which=which: (p, 0, which * pairs + h))
        for which in range(3)
    ]


def at_pack(*shape):
    rest = (0,) * len(shape)
    return pl.BlockSpec((1, *shape), lambda p, h, place: (jnp.bitwise_xor(p, place[2]), *rest))


def attention(place, qkv, blocks, seg_col, seg_row):
    packs, seq, width = qkv.shape
    width //= 3
    rows, pairs = seq // blocks, width // PAIR
    return pl.pallas_call(
        functools.partial(attend_kernel, blocks),
        grid_spec=pltpu.PrefetchScalarGridSpec(
            num_scalar_prefetch=1,
            grid=(packs, pairs),
            in_specs=[*qkv_parts(seq, pairs), at_pack(seq, 1), at_pack(1, seq)],
            out_specs=[
                pl.BlockSpec(
                    (1, blocks, rows, PAIR), lambda p, h, place: (jnp.bitwise_xor(p, place[2]), 0, 0, h)
                ),
                pl.BlockSpec((2, 1, 2, rows, PAIR), lambda p, h, place: (0, p, 0, 0, h)),
                pl.BlockSpec((1, 1, 2, seq), lambda p, h, place: (p, h, 0, 0)),
            ],
        ),
        out_shape=[
            jax.ShapeDtypeStruct((packs, blocks, rows, width), bf16),
            jax.ShapeDtypeStruct((2, packs, 2, rows, width), bf16),
            jax.ShapeDtypeStruct((packs, pairs, 2, seq), f32),
        ],
        **limits(16),
    )(place, qkv, qkv, qkv, seg_col, seg_row)


def attention_back(place, qkv, grad, totals, cosine, sine, seg_col, seg_row, time=25):
    packs, blocks, rows, width = grad.shape
    pairs, seq = width // PAIR, blocks * rows
    return pl.pallas_call(
        functools.partial(attend_back_kernel, blocks),
        grid_spec=pltpu.PrefetchScalarGridSpec(
            num_scalar_prefetch=1,
            grid=(packs, pairs),
            in_specs=[
                *qkv_parts(seq, pairs),
                pl.BlockSpec(
                    (1, blocks, rows, PAIR), lambda p, h, place: (jnp.bitwise_xor(p, place[2]), 0, 0, h)
                ),
                pl.BlockSpec((1, 1, 2, seq), lambda p, h, place: (p, h, 0, 0)),
                at_pack(seq, PAIR), at_pack(seq, PAIR), at_pack(seq, 1), at_pack(1, seq),
            ],
            out_specs=pl.BlockSpec((2, 1, 2, rows, 3 * width), lambda p, h, place: (0, p, 0, 0, 0)),
            scratch_shapes=[pltpu.VMEM((seq, PAIR), f32)] * 2,
        ),
        out_shape=jax.ShapeDtypeStruct((2, packs, 2, rows, 3 * width), bf16),
        **limits(time),
    )(place, qkv, qkv, qkv, grad, totals, cosine, sine, seg_col, seg_row)


def norm_kernel(*refs):
    *piece_refs, gain_ref, shift_ref, act_ref = refs
    step, at = 64, 0
    for piece in piece_refs:
        for row in range(0, piece.shape[0], step):
            normed = layer_stats(piece[row : row + step, :].astype(f32))[0]
            act_ref[at : at + step, :] = (normed * gain_ref[...] + shift_ref[...]).astype(bf16)
            at += step


def norm_rows(pieces, gain, shift):
    count, width = sum(piece.shape[0] for piece in pieces), gain.shape[1]
    return pl.pallas_call(
        norm_kernel,
        out_shape=jax.ShapeDtypeStruct((count, width), bf16),
        **limits(7),
    )(*pieces, gain, shift)


def pick(halves, steps):
    return jnp.where(pl.program_id(0) < steps // 2, halves[0][...], halves[1][...])


def project_kernel(place, act0_ref, act1_ref, weight_ref, bias_ref, cos_ref, sin_ref, out_ref):
    act = pick((act0_ref, act1_ref), 8)
    projected = nn(act, weight_ref[...]) + bias_ref[...]
    rows, width = projected.shape
    first = lanes_of(rows) % HEAD_DIM < ROT_DIMS // 2
    cosine, sine = cos_ref[0], sin_ref[0]
    for at in range(0, width, PAIR):
        part = projected[:, at : at + PAIR]
        if at < 2 * width // 3:
            part = turned(part, cosine, sine, first)
        out_ref[0, :, at : at + PAIR] = part.astype(bf16)


def project(place, act, weight, bias, cosine, sine):
    count, depth = act[0].shape
    width = weight.shape[1]
    packs, seq, _ = cosine.shape
    rows = count // 4

    def block_of(s, place):
        return jnp.bitwise_xor(place[0], s % 2) * 2 + jnp.bitwise_xor(place[1], s // 4)

    def table(s, place):
        return (jnp.bitwise_xor(place[2], s // 2 % 2), block_of(s, place), 0)

    return pl.pallas_call(
        project_kernel,
        grid_spec=pltpu.PrefetchScalarGridSpec(
            num_scalar_prefetch=1,
            grid=(8,),
            in_specs=[
                *half_specs(rows, depth),
                pl.BlockSpec((depth, width), lambda s, place: (0, 0)),
                pl.BlockSpec((1, width), lambda s, place: (0, 0)),
                pl.BlockSpec((1, rows, PAIR), table),
                pl.BlockSpec((1, rows, PAIR), table),
            ],
            out_specs=pl.BlockSpec((1, rows, width), lambda s, place: (s // 2 % 2, block_of(s, place), 0)),
        ),
        out_shape=jax.ShapeDtypeStruct((packs, seq, width), bf16),
        **limits(15),
    )(place, *act, weight, bias, cosine, sine)


def slot_of(s, place):
    return jnp.bitwise_xor(place[3], s // 4 + (s // 2 % 2) * 4 + (s % 2) * 2)


def half_specs(rows, width, steps=8):
    half = steps // 2
    return [
        pl.BlockSpec((rows, width), lambda s, *place: (jnp.minimum(s, half - 1), 0)),
        pl.BlockSpec((rows, width), lambda s, *place: (jnp.maximum(s - half, 0), 0)),
    ]


def out_kernel(place, mixed_ref, w0_ref, w1_ref, token_ref, gain_ref, shift_ref, hidden_ref, act_ref, sum_ref):
    s = pl.program_id(0)

    @pl.when(s == 0)
    def _():
        sum_ref[...] = token_ref[...].astype(f32)

    @pl.when(s < 4)
    def _():
        sum_ref[...] += nn(mixed_ref[0], w0_ref[...])

    @pl.when(s >= 4)
    def _():
        sum_ref[...] += nn(mixed_ref[0], w1_ref[...])

    @pl.when(s == 7)
    def _():
        hidden = sum_ref[...]
        hidden_ref[...] = hidden
        act_ref[...] = (layer_stats(hidden)[0] * gain_ref[...] + shift_ref[...]).astype(bf16)


def out_rows_of(place, mixed, weight, tokens, gain, shift):
    rows, width = tokens.shape
    part = mixed.shape[2]
    whole = pl.BlockSpec((rows, width), lambda s, place: (0, 0))
    vector = pl.BlockSpec((1, width), lambda s, place: (0, 0))
    return pl.pallas_call(
        out_kernel,
        grid_spec=pltpu.PrefetchScalarGridSpec(
            num_scalar_prefetch=1,
            grid=(8,),
            in_specs=[
                pl.BlockSpec((1, rows, part), lambda s, place: (slot_of(s, place), 0, 0)),
                *half_specs(part, width), whole, vector, vector,
            ],
            out_specs=[whole, whole],
            scratch_shapes=[pltpu.VMEM((rows, width), f32)],
        ),
        out_shape=[jax.ShapeDtypeStruct((rows, width), f32), jax.ShapeDtypeStruct((rows, width), bf16)],
        **limits(12),
    )(place, mixed, *weight, tokens, gain, shift)


def out_back_kernel(
    place, own_ref, x_ref, y_ref, far_ref, hidden_ref, grad_ref, gain_ref, w0_ref, w1_ref,
    mixed_ref, total_ref, low_ref, vector_ref,
):
    s = pl.program_id(0)

    @pl.when(s == 0)
    def _():
        norm_grad = own_ref[...] + x_ref[...].astype(f32) + y_ref[...].astype(f32) + far_ref[...].astype(f32)
        normed, inv_std = layer_stats(hidden_ref[...])
        vector_ref[0:1, :] = jnp.sum(norm_grad * normed, axis=0, keepdims=True)
        vector_ref[1:2, :] = jnp.sum(norm_grad, axis=0, keepdims=True)
        total = grad_ref[...].astype(f32) + norm_back(norm_grad, normed, inv_std, gain_ref[...])
        total_ref[...] = total
        low_ref[...] = total.astype(bf16)

    @pl.when(s < 4)
    def _():
        mixed_ref[0] = nt(low_ref[...], w0_ref[...]).astype(bf16)

    @pl.when(s >= 4)
    def _():
        mixed_ref[0] = nt(low_ref[...], w1_ref[...]).astype(bf16)


def out_back_rows(place, terms, hidden, out_grad, gain, weight, time=15):
    rows, width = hidden.shape
    part = weight[0].shape[0] // 4
    whole = pl.BlockSpec((rows, width), lambda s, place: (0, 0))
    vector = pl.BlockSpec((1, width), lambda s, place: (0, 0))
    return pl.pallas_call(
        out_back_kernel,
        grid_spec=pltpu.PrefetchScalarGridSpec(
            num_scalar_prefetch=1,
            grid=(8,),
            in_specs=[*[whole] * 6, vector, *half_specs(part, width)],
            out_specs=[
                pl.BlockSpec((1, rows, part), lambda s, place: (slot_of(s, place), 0, 0)),
                whole, whole, pl.BlockSpec((2, width), lambda s, place: (0, 0)),
            ],
        ),
        out_shape=[
            jax.ShapeDtypeStruct((8, rows, part), bf16),
            jax.ShapeDtypeStruct((rows, width), f32),
            jax.ShapeDtypeStruct((rows, width), bf16),
            jax.ShapeDtypeStruct((2, width), f32),
        ],
        **limits(time),
    )(place, *terms, hidden, out_grad, gain, *weight)


STEPS = 4


def gate_kernel(act0_ref, act1_ref, weight_ref, middle_ref, by_gate_ref, by_up_ref):
    act = pick((act0_ref, act1_ref), STEPS)
    both = nn(act, weight_ref[...])
    half, wide = both.shape[1] // 2, middle_ref.shape[1]
    inside = lax.broadcasted_iota(jnp.int32, (both.shape[0], wide), 1) < half
    gate = jnp.where(inside, both[:, :wide], 0.0)
    up = jnp.where(inside, pltpu.roll(both[:, 2 * half - wide :], half, 1), 0.0)
    sigmoid = jax.nn.sigmoid(gate)
    silu = gate * sigmoid
    middle_ref[...] = (silu * up).astype(bf16)
    by_gate_ref[...] = (up * (sigmoid * (1.0 + gate * (1.0 - sigmoid)))).astype(bf16)
    by_up_ref[...] = silu.astype(bf16)


def gate_rows(act, weight, half):
    count, depth = act[0].shape
    count *= 2
    wide, rows = -(-half // PAIR) * PAIR, count // STEPS
    out = pl.BlockSpec((rows, wide), lambda s: (s, 0))
    return pl.pallas_call(
        gate_kernel,
        grid=(STEPS,),
        in_specs=[*half_specs(rows, depth, STEPS), pl.BlockSpec((depth, 2 * half), lambda s: (0, 0))],
        out_specs=[out] * 3,
        out_shape=[jax.ShapeDtypeStruct((count, wide), bf16)] * 3,
        **limits(20),
    )(*act, weight)


def gate_back_kernel(grad0_ref, grad1_ref, weight_ref, by_gate_ref, by_up_ref, out_ref):
    middle = nn(pick((grad0_ref, grad1_ref), STEPS), weight_ref[...])
    gate = middle * by_gate_ref[...].astype(f32)
    half, wide = out_ref.shape[1] // 2, middle.shape[1]
    up = pltpu.roll(middle * by_up_ref[...].astype(f32), half - (2 * half - wide), 1)
    cut = 2 * half - wide
    out_ref[:, :cut] = gate[:, :cut].astype(bf16)
    out_ref[:, cut:wide] = (gate[:, cut:] + up[:, : wide - cut]).astype(bf16)
    out_ref[:, wide:] = up[:, wide - cut :].astype(bf16)


def gate_back_rows(grad, weight, by_gate, by_up, half):
    count, depth = grad[0].shape
    count *= 2
    wide, rows = by_gate.shape[1], count // STEPS
    part = pl.BlockSpec((rows, wide), lambda s: (s, 0))
    return pl.pallas_call(
        gate_back_kernel,
        grid=(STEPS,),
        in_specs=[
            *half_specs(rows, depth, STEPS), columns_of(weight, 2 * half, wide), part, part
        ],
        out_specs=pl.BlockSpec((rows, 2 * half), lambda s: (s, 0)),
        out_shape=jax.ShapeDtypeStruct((count, 2 * half), bf16),
        **limits(13),
    )(*grad, weight, by_gate, by_up)


def halves(low_part, low_at, high_part, high_at):
    low_part = low_part if low_at == 0 else pltpu.roll(low_part, HEAD_DIM, 1)
    high_part = high_part if high_at else pltpu.roll(high_part, HEAD_DIM, 1)
    return jnp.where(lanes_of(low_part.shape[0]) < HEAD_DIM, low_part, high_part)


def lane_group(load, at):
    return load(at // PAIR * PAIR), at % PAIR


def split_heads_kernel(team, weight_ref, out_ref):
    def load(at):
        return weight_ref[:, at : at + PAIR].astype(f32)

    chunks = weight_ref.shape[1] // (team * HEAD_DIM)
    for p in range(team):
        for chunk in range(0, chunks, 2):
            low = lane_group(load, (chunk * team + p) * HEAD_DIM)
            high = lane_group(load, ((chunk + 1) * team + p) * HEAD_DIM)
            out_ref[p, :, chunk * HEAD_DIM : (chunk + 2) * HEAD_DIM] = halves(*low, *high).astype(bf16)


def split_heads(weight, team):
    rows, width = weight.shape
    return pl.pallas_call(
        functools.partial(split_heads_kernel, team),
        out_shape=jax.ShapeDtypeStruct((team, rows, width // team), bf16),
        **limits(2),
    )(weight)


def merge_heads_kernel(part_ref, out_ref):
    team = part_ref.shape[0]
    chunks = part_ref.shape[2] // HEAD_DIM
    for chunk in range(chunks):
        for p in range(0, team, 2):
            at = chunk * HEAD_DIM

            def load(at, p=p):
                return part_ref[p, :, at : at + PAIR].astype(f32)

            def load_next(at, p=p):
                return part_ref[p + 1, :, at : at + PAIR].astype(f32)

            to = (chunk * team + p) * HEAD_DIM
            out_ref[:, to : to + PAIR] = halves(*lane_group(load, at), *lane_group(load_next, at))


def merge_heads(parts):
    team, rows, width = parts.shape
    return pl.pallas_call(
        merge_heads_kernel,
        out_shape=jax.ShapeDtypeStruct((rows, team * width), f32),
        **limits(2),
    )(parts)


def split_ffn_kernel(team, my_ffn, *refs):
    *weight_refs, out_ref = refs
    steps = my_ffn // HEAD_DIM

    def chunk(p, at):
        which, inside = at // steps, at % steps * HEAD_DIM
        if which == len(weight_refs):
            return jnp.zeros((out_ref.shape[1], PAIR), f32), at % 2 * HEAD_DIM
        return lane_group(
            lambda lane: weight_refs[which][:, lane : lane + PAIR].astype(f32), p * my_ffn + inside
        )

    for p in range(team):
        for at in range(0, out_ref.shape[2], PAIR):
            first = at // HEAD_DIM
            out_ref[p, :, at : at + PAIR] = halves(*chunk(p, first), *chunk(p, first + 1)).astype(bf16)


def split_ffn(weights, team, packed):
    rows, width = weights[0].shape
    return pl.pallas_call(
        functools.partial(split_ffn_kernel, team, width // team),
        out_shape=jax.ShapeDtypeStruct((team, rows, packed), bf16),
        **limits(3),
    )(*weights)


def merge_ffn_kernel(my_ffn, part_ref, *out_refs):
    team = part_ref.shape[0]
    for which, out_ref in enumerate(out_refs):

        def chunk(at):
            p, inside = at // my_ffn, at % my_ffn
            group, lane = (which * my_ffn + inside) // PAIR * PAIR, (which * my_ffn + inside) % PAIR
            return part_ref[p, :, group : group + PAIR].astype(f32), lane

        for at in range(0, team * my_ffn, PAIR):
            out_ref[:, at : at + PAIR] = halves(*chunk(at), *chunk(at + HEAD_DIM))


def merge_ffn(parts, count, ffn):
    team, rows, width = parts.shape
    parts = jnp.pad(parts, ((0, 0), (0, 0), (0, -width % PAIR)))
    return pl.pallas_call(
        functools.partial(merge_ffn_kernel, ffn // team),
        out_shape=[jax.ShapeDtypeStruct((rows, ffn), f32)] * count,
        **limits(3),
    )(parts)


def local(
    tokens, segments, positions, out_grad, ln1_gain, ln1_bias, qkv_weight, qkv_bias, o_weight,
    ln2_gain, ln2_bias, gate_weight, up_weight, down_weight,
):
    rows, width = tokens.shape
    shard = qkv_weight.shape[0]
    ffn = gate_weight.shape[1]
    heads = width // HEAD_DIM
    team = lax.axis_size(PLANE)
    depth = lax.axis_size("g")
    devices = team * depth
    packs = lax.axis_size("y")
    blocks = team // packs
    seq = blocks * rows
    my_heads = heads // team
    my_width = my_heads * HEAD_DIM
    my_ffn = ffn // team
    packed = -(-3 * my_ffn // PAIR) * PAIR
    me = lax.axis_index(PLANE)
    place = jnp.stack(
        [lax.axis_index("x"), lax.axis_index("c"), lax.axis_index("y"), me]
    ).astype(jnp.int32)
    aligned = shard == HEAD_DIM

    vectors = jnp.stack([ln1_gain, ln1_bias, ln2_gain, ln2_bias], axis=0)
    vectors = jnp.concatenate([vectors, jnp.transpose(qkv_bias)], axis=0).astype(f32).reshape(-1)
    small = jnp.concatenate([vectors, segments.astype(f32), positions.astype(f32)])
    small = lax.all_to_all(
        jnp.broadcast_to(small[None], (devices, small.shape[0])), ALL, 0, 0, tiled=True
    )
    vectors = jnp.transpose(small[:, : 7 * shard].reshape(devices, 7, shard), (1, 0, 2)).reshape(7, width)
    gain_one, shift_one, gain_two, shift_two = (vectors[i][None, :] for i in range(4))
    my_plane = lax.dynamic_slice_in_dim(small[:, 7 * shard :], lax.axis_index("g") * team, team, 0)
    segment_all = my_plane[:, :rows].reshape(packs, seq)
    position_all = my_plane[:, rows:].reshape(packs, seq)
    bias_mine = lax.dynamic_slice_in_dim(
        vectors[4:7].reshape(3, my_heads, team, HEAD_DIM), me, 1, 2
    ).reshape(1, 3 * my_width)

    token_pieces = chip_pieces(tokens)
    qkv_send = after(split_heads(qkv_weight, team), small)
    qkv_mine = plane_all_to_all(qkv_send).reshape(team * shard, 3 * my_width)
    ffn_send = split_ffn([gate_weight, up_weight, down_weight], team, packed)
    ffn_send = after(ffn_send, qkv_mine, *token_pieces)
    ffn_mine = plane_all_to_all(ffn_send).reshape(team * shard, packed)

    frequency = rope_base ** (-jnp.arange(0, ROT_DIMS, 2, dtype=f32) / ROT_DIMS)
    within = jnp.arange(PAIR) % HEAD_DIM
    phases = position_all[:, :, None] * jnp.where(within < ROT_DIMS, frequency[within % (ROT_DIMS // 2)], 0.0)
    cosine = jnp.cos(phases)
    sine = jnp.sin(phases) * jnp.where(within < ROT_DIMS // 2, -1.0, 1.0)
    seg_col, seg_row = segment_all[:, :, None], segment_all[:, None, :]

    def over_g(piece):
        return lax.all_gather(piece, "g", axis=0, tiled=True)

    act_one = norm_rows(token_pieces, gain_one, shift_one)
    ffn_mine = after(ffn_mine, act_one, cosine, sine, seg_col)
    act_one = act_one, swap(act_one, "c")
    if aligned:
        out_rows = after(over_g(o_weight), ffn_mine, act_one[0])
    else:
        out_abs = lax.all_gather(o_weight, ALL, axis=0, tiled=True)
        out_abs = out_abs.reshape(my_heads, team, HEAD_DIM, width)
        out_full = [
            jnp.concatenate(
                [jnp.take(out_abs, slot_of(s, place), axis=1).reshape(my_width, width) for s in span], axis=0
            )
            for span in (range(4), range(4, 8))
        ]
    qkv_full = over_g(qkv_mine)
    ffn_full = over_g(ffn_mine)
    qkv_full = after(qkv_full, act_one[0], ffn_mine)

    qkv = project(place, act_one, qkv_full, bias_mine, cosine, sine)
    mixed, mixed_halves, totals = attention(place, qkv, blocks, seg_col, seg_row)
    if aligned:
        out_full = halves_of(chip_pieces(out_rows, qkv), mixed)
    hidden, act_two = out_rows_of(
        place, plane_all_to_all(mixed.reshape(team, rows, my_width)), out_full, tokens, gain_two, shift_two
    )

    act_two = halves_of(chip_pieces(act_two))
    cotangent = chip_pieces(after(out_grad, act_two[0]))
    middle_low, by_gate, by_up = gate_rows(act_two, ffn_full, my_ffn)
    cotangent = halves_of(cotangent, middle_low)
    output_other = swap(plane_send(middle_low, ffn_full, 2 * my_ffn), "c")
    down_sum = row_sum(cotangent, middle_low, kept=my_ffn)
    output_kept = plane_keep(after(middle_low, down_sum), ffn_full, 2 * my_ffn, output_other)

    def own_rows(grad_sum):
        return lax.psum_scatter(grad_sum, "g", scatter_dimension=0, tiled=True)

    def back_to_rows(columns):
        return plane_all_to_all(columns.reshape(team, shard, columns.shape[1]))

    down_own = own_rows(down_sum)
    gate_up_grad = gate_back_rows(after(cotangent, output_kept[0]), ffn_full, by_gate, by_up, my_ffn)
    output_terms = after(plane_corner(output_kept), gate_up_grad)
    norm_two_other = swap(plane_send(after(gate_up_grad, output_terms[0]), ffn_full, 0), "c")
    norm_two_kept = plane_keep(gate_up_grad, ffn_full, 0, norm_two_other, bf16)
    gate_up_sum = row_sum(act_two, after(gate_up_grad, norm_two_kept[0], down_own), time=60)
    output = (hidden + total_of(after(plane_neighbours(output_terms), gate_up_sum))).astype(bf16)
    gate_up_own = own_rows(gate_up_sum)
    norm_two_terms = after(plane_direct(norm_two_kept), output)
    mixed_grad, hidden_grad, hidden_low, two_sums = out_back_rows(
        place, norm_two_terms, hidden, out_grad, gain_two, out_full, time=130
    )
    down_recv = back_to_rows(after(down_own, norm_two_terms))

    mixed_grad = plane_all_to_all(after(mixed_grad, down_recv)).reshape(packs, blocks, rows, my_width)
    qkv_grad = attention_back(place, qkv, mixed_grad, totals, cosine, sine, seg_col, seg_row, time=130)
    qkv_grad = qkv_grad.reshape(8 * rows, 3 * my_width)
    hidden_pieces = chip_pieces(after(hidden_low, mixed_grad), qkv_grad)
    qkv_sum = row_sum(act_one, after(qkv_grad, hidden_pieces[1]), time=130)
    qkv_own = own_rows(qkv_sum)
    norm_one_sent = plane_send(after(qkv_grad, qkv_sum, hidden_pieces), qkv_full, 0, time=60)
    norm_one_other = swap(norm_one_sent, "c")
    hidden_all = halves_of(hidden_pieces, norm_one_other, time=60)
    gate_up_recv = back_to_rows(after(gate_up_own, norm_one_other))
    norm_one_kept = plane_keep(after(qkv_grad, hidden_all[0]), qkv_full, 0, norm_one_other, bf16)
    mixed_halves = mixed_halves.reshape(2, 4 * rows, my_width)
    out_sum = pair_sum(mixed_halves, after(hidden_all, norm_one_kept[0], gate_up_recv), time=60)
    if aligned:
        out_share = own_rows(out_sum).astype(f32)
    else:
        spread = jnp.zeros((my_heads, team, HEAD_DIM, width), bf16)
        spread = lax.dynamic_update_slice_in_dim(
            spread, out_sum.reshape(my_heads, 1, HEAD_DIM, width), me, 1
        )
        out_share = lax.psum_scatter(
            spread.reshape(width, width).astype(f32), ALL, scatter_dimension=0, tiled=True
        )
    norm_one_terms = after(plane_direct(norm_one_kept), out_sum)
    qkv_recv = back_to_rows(after(qkv_own, out_sum))
    norm_grad_one = total_of(after(norm_one_terms, qkv_recv))
    normed_one, inv_one = layer_stats(tokens.astype(f32))
    input_grad = (hidden_grad + norm_back(norm_grad_one, normed_one, inv_one, gain_one)).astype(bf16)
    down_share = merge_ffn(after(down_recv, out_sum), 1, ffn)
    gate_up_share = merge_ffn(gate_up_recv, 2, ffn)

    bias_sum = jnp.sum(qkv_grad.astype(f32), axis=0).reshape(3, my_heads, 1, HEAD_DIM)
    mine = (jnp.arange(team) == me).astype(f32)[None, None, :, None]
    terms = jnp.concatenate(
        [
            jnp.sum(norm_grad_one * normed_one, axis=0)[None],
            jnp.sum(norm_grad_one, axis=0)[None],
            (bias_sum * mine).reshape(3, width),
            two_sums,
        ],
        axis=0,
    )
    terms = jnp.transpose(terms.reshape(7, devices, shard), (1, 0, 2)).reshape(devices, 7 * shard)
    vector_share = jnp.sum(lax.all_to_all(terms, ALL, 0, 0, tiled=True), axis=0).reshape(7, shard)
    qkv_share = merge_heads(qkv_recv)
    return (
        output,
        input_grad,
        vector_share[0],
        vector_share[1],
        qkv_share,
        jnp.transpose(vector_share[2:5]),
        out_share,
        vector_share[5],
        vector_share[6],
        *gate_up_share,
        *down_share,
    )


def solution(mesh):
    dp, ctx = mesh.shape["dp"], mesh.shape["ctx"]
    split = Mesh(mesh.devices.reshape(dp // 2, 2, ctx // 2, 2), ALL)
    row, flat = P(ALL, None), P(ALL)
    return jax.shard_map(
        local,
        mesh=split,
        in_specs=(row, flat, flat, row, flat, flat, row, row, row, flat, flat, row, row, row),
        out_specs=(row, row, flat, flat, row, row, row, flat, flat, row, row, row),
        check_vma=False,
    )
```
